128 devices in a mesh: span: 4 (over z), dom: 32 (over y, x, core).
Axes of the slice: x: 4, y: 4, z: 4, core: 2. Of those that a mesh axis runs over, the one named last changes fastest.
Arguments:
- adjoint_rhs: float32 [6, 128, 32768], P(None, 'span', 'dom'), may hold values from -6 to 6
- block_inverse: float32 [6, 6, 128, 32768], P(None, None, 'span', 'dom')
- coupling: float32 [4, 128, 32768], P(None, 'span', 'dom'), may hold values from 0.05 to 0.25
- distance_grad: float32 [1, 128, 32768], P(None, 'span', 'dom'), may hold values from -6 to 6
- slot_cell: int32 [4, 32, 65536], P('span', 'dom'), may hold values from 0 to 32768, as said below
- slot_face: int32 [4, 32, 65536], P('span', 'dom'), may hold values from 0 to 8192, as said below
- area_grad: float32 [3, 4, 262144], P(None, None, 'dom'), may hold values from -6 to 6
- face_nodes: int32 [4, 262144], P(None, 'dom'), may hold values from 0 to 131071, as said below
Outputs:
- adjoint: float32 [6, 128, 32768], P(None, 'span', 'dom')
- face_sens: float32 [262144], P('dom')
- node_sens: float32 [3, 131072], P(None, 'dom')
The draws below stay inside these ranges and needn't reach their ends.
Inputs may be any that keep to these rules, and one draw needn't show every extreme that they name: `slot_cell`: entry [s, i, j * 2048 + k] is a local cell of device (s, i) sent to face owner j, or the pad 32768; each owner's live slots come first, every local cell stands in exactly one slot, and one owner has all 2048 slots live from every device. `slot_face`: entry [s, j, i * 2048 + k] is the owner-local wall face of owner j nearest to the cell in slot j * 2048 + k of device (s, i), and is the pad 8192 exactly where that slot is a pad. `face_nodes`: node n is owned by dom index n // 4096; the nodes of face g are owned by dom index i = g // 8192, by one of its two neighbours, or by the index i + 16, all counted periodically along dom.
All inputs are finite; a program needn't handle non-finite values.
Results may differ from the reference program's by a relative error of at most 0.00011.
Values sent between devices are 32-bit elements; how exact they have to be, the bound alone decides.
No kernel may reach another device: no remote copies, remote signals or barrier semaphores. Data moves between devices by JAX's collectives and lax.ppermute only.
A program may use at most 192 MiB of HBM per device.

```python
import jax
import jax.numpy as jnp
from jax import lax

NVAR = 6
SWEEPS = 4
CX = 32
CY = 1024
FACE_DEV = 8192
NODE_DEV = 4096
CELLS = 32768
CAP = 2048
NX = 128
NY = 32768
FACES = 262144
NODES = 131072
N_SPAN = 4
N_DOM = 32


def slot_tables(key):
    key_perm = jax.random.fold_in(key, 101)
    key_pair = jax.random.fold_in(key, 102)
    key_cells = jax.random.fold_in(key, 103)
    key_heavy = jax.random.fold_in(key, 104)
    key_narrow = jax.random.fold_in(key, 105)
    key_wide = jax.random.fold_in(key, 106)
    owner_perm = jax.random.permutation(key_perm, N_DOM)
    inverse_perm = jnp.argsort(owner_perm)
    extra = jax.random.randint(key_pair, (N_SPAN, N_DOM, N_DOM // 2), 0, CAP // 2 + 1)
    extra = extra.at[:, :, 0].set(CAP // 2)
    paired = jnp.stack([CAP // 2 + extra, CAP // 2 - extra], axis=-1).reshape(N_SPAN, N_DOM, N_DOM)
    counts = paired[:, :, inverse_perm]
    live = jnp.arange(CAP).reshape(1, 1, 1, CAP) < counts[:, :, :, None]
    offsets = jnp.cumsum(counts, axis=-1) - counts
    position = (offsets[:, :, :, None] + jnp.arange(CAP).reshape(1, 1, 1, CAP)).reshape(N_SPAN, N_DOM, N_DOM * CAP)
    position = jnp.clip(position, 0, CELLS - 1)
    perms = jax.vmap(lambda k: jax.random.permutation(k, CELLS))(jax.random.split(key_cells, N_SPAN * N_DOM))
    perms = perms.reshape(N_SPAN, N_DOM, CELLS)
    cells = jnp.take_along_axis(perms, position, axis=2).reshape(N_SPAN, N_DOM, N_DOM, CAP)
    cells = jnp.where(live, cells, CELLS).astype(jnp.int32)
    heavy = jax.random.randint(key_heavy, (N_SPAN, N_DOM, N_DOM, CAP), 0, 4) == 0
    narrow = jax.random.randint(key_narrow, (N_SPAN, N_DOM, N_DOM, CAP), 0, max(FACE_DEV // 16, 1))
    wide = jax.random.randint(key_wide, (N_SPAN, N_DOM, N_DOM, CAP), 0, FACE_DEV)
    faces = jnp.where(live, jnp.where(heavy, narrow, wide), FACE_DEV).astype(jnp.int32)
    return (cells, faces)


def draw_slot_cell(key, part):
    cells, faces = slot_tables(key)
    return cells.reshape(N_SPAN, N_DOM, N_DOM * CAP)


def draw_slot_face(key, part):
    cells, faces = slot_tables(key)
    return faces.transpose(0, 2, 1, 3).reshape(N_SPAN, N_DOM, N_DOM * CAP)


def draw_face_nodes(key, part):
    key = jax.random.fold_in(key, 7)
    key_side = jax.random.fold_in(key, 1)
    key_node = jax.random.fold_in(key, 2)
    owner = (jnp.arange(FACES, dtype=jnp.int32) // FACE_DEV).reshape(1, FACES)
    side = jax.random.randint(key_side, (4, FACES), 0, 5)
    delta = jnp.where(side == 2, -1, jnp.where(side == 3, 1, jnp.where(side == 4, N_DOM // 2, 0)))
    target = (owner + delta + N_DOM) % N_DOM
    local = jax.random.randint(key_node, (4, FACES), 0, NODE_DEV)
    return (target * NODE_DEV + local).astype(jnp.int32)


def draw_block_inverse(key, part):
    key = jax.random.fold_in(key, 11)
    key_diag = jax.random.fold_in(key, 1)
    key_off = jax.random.fold_in(key, 2)
    low = jnp.log(0.3)
    high = jnp.log(1.0)
    diagonal = jnp.exp(jax.random.uniform(key_diag, (NVAR, NX, NY), jnp.float32, low, high))
    off = 0.06 * jax.random.normal(key_off, (NVAR, NVAR, NX, NY), jnp.float32)
    unit = jnp.eye(NVAR, dtype=jnp.float32).reshape(NVAR, NVAR, 1, 1)
    return (unit * diagonal[None, :, :, :] + (1.0 - unit) * off).astype(jnp.float32)


def levels(rng, shape, cuts, smallest, top_value):
    level = 1.0
    for axis_at, parts in cuts:
        heights = jax.random.uniform(jax.random.fold_in(jax.random.fold_in(rng, 6), axis_at), (parts,), jnp.float32, smallest / len(cuts), top_value / len(cuts))
        level = level * jnp.repeat(jnp.exp(heights), shape[axis_at] // parts).reshape((-1,) + (1,) * (len(shape) - 1 - axis_at))
    return level


def bell_draw(own_key, extent, scale, limit, cuts=(), held_as=jnp.bfloat16):
    result = scale * jax.random.normal(own_key, extent, jnp.float32)
    if cuts:
        result = result * levels(own_key, extent, cuts, -0.22, 0.18)
    return jnp.clip(result, -limit, limit).astype(held_as)


def setup_inputs(seed: int = 0) -> dict:
    streams_of = jax.random.split(jax.random.key(seed), 9)
    return {
        "adjoint_rhs": bell_draw(streams_of[0], (NVAR, NX, NY), 1.0, 6.0, ((1, 4), (2, 32)), jnp.float32),
        "block_inverse": draw_block_inverse(jax.random.fold_in(streams_of[8], 71), 0),
        "coupling": jnp.clip(0.05 + 0.2 * jax.random.uniform(streams_of[2], (4, NX, NY), jnp.float32) ** levels(streams_of[2], (4, NX, NY), ((1, 4), (2, 32)), -0.2, 0.2), 0.05, 0.25),
        "distance_grad": bell_draw(streams_of[3], (1, NX, NY), 1.0, 6.0, ((1, 4), (2, 32)), jnp.float32),
        "slot_cell": draw_slot_cell(jax.random.fold_in(streams_of[8], 71), 0),
        "slot_face": draw_slot_face(jax.random.fold_in(streams_of[8], 71), 0),
        "area_grad": bell_draw(streams_of[6], (3, 4, FACES), 1.0, 6.0, ((2, 32),), jnp.float32),
        "face_nodes": draw_face_nodes(jax.random.fold_in(streams_of[8], 71), 0),
    }


def apply_inverse(inverse, vector):
    return jnp.einsum("baxy,bxy->axy", inverse, vector, precision=lax.Precision.HIGHEST)


def relax_sweep(field, coupling, inverse, objective):
    total = (coupling[1:2] * field)[:, 2:, 1:-1] + (coupling[0:1] * field)[:, :-2, 1:-1]
    total = total + (coupling[3:4] * field)[:, 1:-1, 2:] + (coupling[2:3] * field)[:, 1:-1, :-2]
    return apply_inverse(inverse, objective - total)


def rimmed_global(field):
    padded = jnp.pad(field, ((0, 0), (1, 1), (0, 0)))
    return jnp.concatenate([padded[:, :, -1:], padded, padded[:, :, :1]], axis=2)


def reference(adjoint_rhs, block_inverse, coupling, distance_grad, slot_cell, slot_face, area_grad, face_nodes):
    adjoint = apply_inverse(block_inverse, adjoint_rhs)
    coupling_ext = rimmed_global(coupling)
    for sweep in range(SWEEPS):
        adjoint = relax_sweep(rimmed_global(adjoint), coupling_ext, block_inverse, adjoint_rhs)
    cell_sens = distance_grad[0] * adjoint[NVAR - 1]
    blocks = cell_sens.reshape(N_SPAN, CX, N_DOM, CY).transpose(0, 2, 1, 3).reshape(N_SPAN, N_DOM, CELLS)
    padded = jnp.concatenate([blocks, jnp.zeros((N_SPAN, N_DOM, 1), jnp.float32)], axis=2)
    sent = jnp.take_along_axis(padded, slot_cell, axis=2)
    sent = sent.reshape(N_SPAN, N_DOM, N_DOM, CAP).transpose(0, 2, 1, 3).reshape(N_SPAN, N_DOM, N_DOM * CAP)
    owner = jnp.arange(N_DOM, dtype=jnp.int32).reshape(1, N_DOM, 1)
    global_face = jnp.where(slot_face < FACE_DEV, owner * FACE_DEV + slot_face, FACES).astype(jnp.int32)
    face_sens = jax.ops.segment_sum(sent.reshape(-1), global_face.reshape(-1), FACES + 1)[:FACES]
    contrib = area_grad * face_sens[None, None, :]
    flat_nodes = face_nodes.reshape(-1)
    node_sens = jax.vmap(lambda part: jax.ops.segment_sum(part.reshape(-1), flat_nodes, NODES))(contrib)
    return adjoint, face_sens, node_sens
```

```python
import jax
import jax.numpy as jnp
from jax import lax
from jax.experimental import pallas as pl
from jax.experimental.pallas import tpu as pltpu
from jax.sharding import PartitionSpec as P

NVAR = 6
SWEEPS = 4
CX = 32
CY = 1024
CELLS = 32768
CAP = 2048
FACE_DEV = 8192
NODE_DEV = 4096
N_SPAN = 4
N_DOM = 32
LANES = 128
TILES = CY // LANES
SLOT_ROWS = CAP // LANES
CHUNK_ROWS = 4
CHUNK = CHUNK_ROWS * LANES
FACE_HI = FACE_DEV // LANES
NODE_HI = NODE_DEV // LANES

VMEM = pl.BlockSpec(memory_space=pltpu.VMEM)
SMEM = pl.BlockSpec(memory_space=pltpu.SMEM)
PARAMS = pltpu.CompilerParams(vmem_limit_bytes=40 << 20)
BF = jnp.bfloat16
F32 = jnp.float32


def f32(*shape):
    return jax.ShapeDtypeStruct(shape, F32)


def lane_tile(k):
    return slice(k * LANES, (k + 1) * LANES)


def product(inverse, terms, k):
    out = []
    for a in range(NVAR):
        total = inverse[0, a, :, lane_tile(k)] * terms[0]
        for b in range(1, NVAR):
            total = total + inverse[b, a, :, lane_tile(k)] * terms[b]
        out.append(total)
    return out


def store_edges(values, coupling, k, low, high, left, right):
    for a in range(NVAR):
        low[a : a + 1, lane_tile(k)] = coupling[1, 0:1, lane_tile(k)] * values[a][0:1]
        high[a : a + 1, lane_tile(k)] = coupling[0, CX - 1 : CX, lane_tile(k)] * values[a][CX - 1 :]
    lane = lax.broadcasted_iota(jnp.int32, (CX, LANES), 1)
    if k == 0:
        total = jnp.zeros((CX, LANES), F32)
        for a in range(NVAR):
            edge = coupling[3, :, lane_tile(k)] * values[a]
            total = jnp.where(lane == a, pltpu.roll(edge, a, 1) if a else edge, total)
        left[...] = total
    if k == TILES - 1:
        total = jnp.zeros((CX, LANES), F32)
        for a in range(NVAR):
            edge = coupling[2, :, lane_tile(k)] * values[a]
            total = jnp.where(lane == a, pltpu.roll(edge, a + 1, 1), total)
        right[...] = total


def first_kernel(rhs, inverse, coupling, out, low, high, left, right):
    for edge in (low, high):
        edge[...] = jnp.zeros_like(edge)
    for k in range(TILES):
        values = product(inverse, [rhs[b, :, lane_tile(k)] for b in range(NVAR)], k)
        for a in range(NVAR):
            out[a, :, lane_tile(k)] = values[a]
        store_edges(values, coupling, k, low, high, left, right)


def neighbour_terms(rhs, coupling, field, above, below, after, before):
    at = lax.axis_index("span")
    row = lax.broadcasted_iota(jnp.int32, (CX, LANES), 0)
    lane = lax.broadcasted_iota(jnp.int32, (CX, LANES), 1)
    after_rolled = {}
    before_rolled = {}

    def roll_back(k, b):
        if (k, b) not in after_rolled:
            if k == TILES:
                after_rolled[k, b] = pltpu.roll(after[...], LANES - 1 - b, 1)
            else:
                part = coupling[3, :, lane_tile(k)] * field[b, :, lane_tile(k)]
                after_rolled[k, b] = pltpu.roll(part, LANES - 1, 1)
        return after_rolled[k, b]

    def roll_on(k, b):
        if (k, b) not in before_rolled:
            if k < 0:
                before_rolled[k, b] = pltpu.roll(before[...], LANES - b, 1) if b else before[...]
            else:
                part = coupling[2, :, lane_tile(k)] * field[b, :, lane_tile(k)]
                before_rolled[k, b] = pltpu.roll(part, 1, 1)
        return before_rolled[k, b]

    def tile(k):
        terms = []
        for b in range(NVAR):
            value = field[b, :, lane_tile(k)]
            up = pltpu.roll(coupling[1, :, lane_tile(k)] * value, CX - 1, 0)
            edge = jnp.where(at == N_SPAN - 1, 0.0, above[b : b + 1, lane_tile(k)])
            total = jnp.where(row == CX - 1, edge, up)
            down = pltpu.roll(coupling[0, :, lane_tile(k)] * value, 1, 0)
            edge = jnp.where(at == 0, 0.0, below[b : b + 1, lane_tile(k)])
            total = total + jnp.where(row == 0, edge, down)
            total = total + jnp.where(lane == LANES - 1, roll_back(k + 1, b), roll_back(k, b))
            total = total + jnp.where(lane == 0, roll_on(k - 1, b), roll_on(k, b))
            terms.append(rhs[b, :, lane_tile(k)] - total)
        return terms

    return tile


def sweep_kernel(
    rhs, inverse, coupling, field, above, below, after, before, out, low, high, left, right
):
    for edge in (low, high):
        edge[...] = jnp.zeros_like(edge)
    terms = neighbour_terms(rhs, coupling, field, above, below, after, before)
    for k in range(TILES):
        values = product(inverse, terms(k), k)
        for a in range(NVAR):
            out[a, :, lane_tile(k)] = values[a]
        store_edges(values, coupling, k, low, high, left, right)


def last_kernel(rhs, inverse, coupling, field, above, below, after, before, grad, out, sens):
    terms = neighbour_terms(rhs, coupling, field, above, below, after, before)
    for k in range(TILES):
        values = product(inverse, terms(k), k)
        for a in range(NVAR):
            out[a, :, lane_tile(k)] = values[a]
        sens[:, lane_tile(k)] = grad[0, :, lane_tile(k)] * values[NVAR - 1]


EDGES = (f32(8, CY), f32(8, CY), f32(CX, LANES), f32(CX, LANES))


def shifted(axis, size, step):
    return [(i, (i + step) % size) for i in range(size)]


def exchange(low, high, left, right):
    above = lax.ppermute(low, "span", shifted("span", N_SPAN, -1))
    below = lax.ppermute(high, "span", shifted("span", N_SPAN, 1))
    after = lax.ppermute(left, "dom", shifted("dom", N_DOM, -1))
    before = lax.ppermute(right, "dom", shifted("dom", N_DOM, 1))
    return above, below, after, before


def relax(rhs, inverse, coupling, grad):
    whole = f32(NVAR, CX, CY)
    field, *edges = pl.pallas_call(
        first_kernel,
        out_shape=(whole, *EDGES),
        in_specs=[VMEM] * 3,
        out_specs=[VMEM] * 5,
        compiler_params=PARAMS,
        name="first_product",
    )(rhs, inverse, coupling)
    for sweep in range(SWEEPS - 1):
        field, *edges = pl.pallas_call(
            sweep_kernel,
            out_shape=(whole, *EDGES),
            in_specs=[VMEM] * 8,
            out_specs=[VMEM] * 5,
            compiler_params=PARAMS,
            name="sweep",
        )(rhs, inverse, coupling, field, *exchange(*edges))
    return pl.pallas_call(
        last_kernel,
        out_shape=(whole, f32(CX, CY)),
        in_specs=[VMEM] * 9,
        out_specs=[VMEM] * 2,
        compiler_params=PARAMS,
        name="last_sweep",
    )(rhs, inverse, coupling, field, *exchange(*edges), grad)


def two_parts(value):
    high = value.astype(BF).astype(F32)
    return high, value - high


def rows_of(ref, first, count):
    return jnp.concatenate([ref[pl.ds(first + i, 1), :] for i in range(count)], axis=1)


def sixteen(row):
    return jnp.broadcast_to(row, (16, row.shape[1])).astype(BF)


def matches(index, count):
    index = sixteen(index.astype(F32))
    first = lax.broadcasted_iota(jnp.int32, index.shape, 0)
    return [(first + 16 * k).astype(F32).astype(BF) == index for k in range(count // 16)]


def one_hot(index, count):
    return jnp.concatenate(
        [jnp.where(m, jnp.array(1, BF), jnp.array(0, BF)) for m in matches(index, count)], axis=0
    )


def weighted(index, count, values):
    masks = matches(index, count)
    parts = []
    for value in values:
        for part in two_parts(value):
            part = sixteen(part)
            parts += [jnp.where(m, part, jnp.array(0, BF)) for m in masks]
    return jnp.concatenate(parts, axis=0)


def outer_sum(left, right):
    return lax.dot_general(left, right, (((1,), (1,)), ((), ())), preferred_element_type=F32)


def gather_kernel(live, sens, slots, out, table):
    cells = jnp.concatenate([sens[:, lane_tile(k)] for k in range(TILES)], axis=0).T
    for part, half in enumerate(two_parts(cells)):
        table[part * LANES : (part + 1) * LANES, :] = half.astype(BF)
    place = lax.broadcasted_iota(jnp.int32, (LANES, CHUNK), 0)
    out[...] = jnp.zeros_like(out)

    @pl.loop(0, N_DOM)
    def owner(j):
        @pl.loop(0, live[j])
        def chunk(k):
            first = j * SLOT_ROWS + k * CHUNK_ROWS
            slot = rows_of(slots, first, CHUNK_ROWS)
            high = jnp.where(slot < CELLS, ((slot >> 7) & (TILES - 1)) * CX + (slot >> 10), 512)
            picked = jnp.dot(table[...], one_hot(high, 256), preferred_element_type=F32)
            picked = picked[:LANES] + picked[LANES:]
            value = jnp.sum(
                jnp.where(place == (slot & (LANES - 1)), picked, 0.0), axis=0, keepdims=True
            )
            for i in range(CHUNK_ROWS):
                out[pl.ds(first + i, 1), :] = value[:, lane_tile(i)]


def gather(sens, slots):
    live = jnp.sum(
        (slots.reshape(N_DOM, CAP // CHUNK, CHUNK)[:, :, 0] < CELLS).astype(jnp.int32), axis=1
    )
    return pl.pallas_call(
        gather_kernel,
        out_shape=f32(N_DOM * SLOT_ROWS, LANES),
        in_specs=[SMEM, VMEM, VMEM],
        out_specs=VMEM,
        scratch_shapes=[pltpu.VMEM((2 * LANES, 2 * LANES), BF)],
        compiler_params=PARAMS,
        name="gather_slots",
    )(live, sens, slots)


def face_kernel(values, faces, out, total):
    total[...] = jnp.zeros_like(total)

    @pl.loop(0, N_DOM)
    def sender(j):
        part = None
        for k in range(CAP // CHUNK):
            first = j * SLOT_ROWS + k * CHUNK_ROWS
            face = rows_of(faces, first, CHUNK_ROWS)
            value = rows_of(values, first, CHUNK_ROWS)
            step = outer_sum(
                weighted(face >> 7, FACE_HI, [value]), one_hot(face & (LANES - 1), LANES)
            )
            part = step if part is None else part + step
        total[...] += part

    out[...] = total[:FACE_HI] + total[FACE_HI:]


def face_sums(values, faces):
    return pl.pallas_call(
        face_kernel,
        out_shape=f32(FACE_HI, LANES),
        in_specs=[VMEM] * 2,
        out_specs=VMEM,
        scratch_shapes=[pltpu.VMEM((2 * FACE_HI, LANES), F32)],
        compiler_params=PARAMS,
        name="face_sums",
    )(values, faces)


def node_kernel(part0, part1, part2, part3, grad, nodes, faces, out, total):
    at = lax.axis_index("span")
    offset = jnp.where(at == 0, 0, jnp.where(at == 1, 1, jnp.where(at == 2, N_DOM - 1, N_DOM // 2)))
    base = lax.rem(lax.axis_index("dom") + offset, N_DOM) * NODE_DEV
    faces[...] = (part0[...] + part1[...]) + (part2[...] + part3[...])
    total[...] = jnp.zeros_like(total)

    @pl.loop(0, FACE_DEV // CHUNK)
    def chunk(g):
        sens = rows_of(faces, g * CHUNK_ROWS, CHUNK_ROWS)
        columns = pl.ds(pl.multiple_of(g * CHUNK, CHUNK), CHUNK)
        part = None
        for k in range(4):
            node = nodes[k : k + 1, columns] - base
            values = [grad[c, k : k + 1, columns] * sens for c in range(3)]
            step = outer_sum(
                weighted(node >> 7, NODE_HI, values), one_hot(node & (LANES - 1), LANES)
            )
            part = step if part is None else part + step
        total[...] += part

    for c in range(3):
        high = total[(2 * c) * NODE_HI : (2 * c + 1) * NODE_HI]
        out[c] = high + total[(2 * c + 1) * NODE_HI : (2 * c + 2) * NODE_HI]


def node_sums(parts, grad, nodes):
    return pl.pallas_call(
        node_kernel,
        out_shape=(f32(FACE_HI, LANES), f32(3, NODE_HI, LANES)),
        in_specs=[VMEM] * 6,
        out_specs=[VMEM] * 2,
        scratch_shapes=[pltpu.VMEM((6 * NODE_HI, LANES), F32)],
        compiler_params=PARAMS,
        name="node_sums",
    )(*parts, grad, nodes)


def to_node_owners(turn):
    offsets = (0, 1, N_DOM - 1, N_DOM // 2)
    return [
        (s * N_DOM + d, (s + turn) % N_SPAN * N_DOM + (d + offsets[s]) % N_DOM)
        for s in range(N_SPAN)
        for d in range(N_DOM)
    ]


def shards(
    adjoint_rhs, block_inverse, coupling, distance_grad, slot_cell, slot_face, area_grad, face_nodes
):
    adjoint, cell_sens = relax(adjoint_rhs, block_inverse, coupling, distance_grad)
    slot_vals = gather(cell_sens, slot_cell.reshape(N_DOM * SLOT_ROWS, LANES))
    received = lax.all_to_all(slot_vals, "dom", split_axis=0, concat_axis=0, tiled=True)
    face_part = face_sums(received, slot_face.reshape(N_DOM * SLOT_ROWS, LANES))
    parts = [face_part] + [
        lax.ppermute(face_part, "span", shifted("span", N_SPAN, turn)) for turn in range(1, N_SPAN)
    ]
    face_sens, part = node_sums(parts, area_grad, face_nodes)
    node_sens = sum(
        lax.ppermute(part, ("span", "dom"), to_node_owners(turn)) for turn in range(N_SPAN)
    )
    return (adjoint, face_sens.reshape(FACE_DEV), node_sens.reshape(3, NODE_DEV))


def solution(mesh):
    in_specs = (
        P(None, "span", "dom"),
        P(None, None, "span", "dom"),
        P(None, "span", "dom"),
        P(None, "span", "dom"),
        P("span", "dom", None),
        P("span", "dom", None),
        P(None, None, "dom"),
        P(None, "dom"),
    )
    out_specs = (P(None, "span", "dom"), P("dom"), P(None, "dom"))
    return jax.shard_map(shards, mesh=mesh, in_specs=in_specs, out_specs=out_specs, check_vma=False)
```

```python
import jax
import jax.numpy as jnp
from jax import lax
from jax.experimental import pallas as pl
from jax.experimental.pallas import tpu as pltpu
from jax.sharding import PartitionSpec as P

NVAR = 6
SWEEPS = 4
CX = 32
CY = 1024
CELLS = 32768
CAP = 2048
FACE_DEV = 8192
NODE_DEV = 4096
N_SPAN = 4
N_DOM = 32
LANES = 128
TILES = CY // LANES
SLOT_ROWS = N_DOM * CAP // LANES
LIVE_ROWS = CELLS // LANES + N_DOM
LIVE_PAD = 384
GATHER_ROWS, GATHER_STEPS = 8, 18
FACE_ROWS, FACE_STEPS = 16, 16
NODE_ROWS, NODE_STEPS = 8, 4
FACE_HI = FACE_DEV // LANES
NODE_HI = NODE_DEV // LANES

VMEM = pl.BlockSpec(memory_space=pltpu.VMEM)
SMEM = pl.BlockSpec(memory_space=pltpu.SMEM)
PARAMS = pltpu.CompilerParams(vmem_limit_bytes=40 << 20)
BF = jnp.bfloat16
F32 = jnp.float32


def f32(*shape):
    return jax.ShapeDtypeStruct(shape, F32)


def lane_tile(k):
    return slice(k * LANES, (k + 1) * LANES)


def product(inverse, terms, k):
    out = []
    for a in range(NVAR):
        total = inverse[0, a, :, lane_tile(k)] * terms[0]
        for b in range(1, NVAR):
            total = total + inverse[b, a, :, lane_tile(k)] * terms[b]
        out.append(total)
    return out


def store_edges(values, coupling, k, low, high, left, right):
    for a in range(NVAR):
        low[a : a + 1, lane_tile(k)] = coupling[1, 0:1, lane_tile(k)] * values[a][0:1]
        high[a : a + 1, lane_tile(k)] = coupling[0, CX - 1 : CX, lane_tile(k)] * values[a][CX - 1 :]
    lane = lax.broadcasted_iota(jnp.int32, (CX, LANES), 1)
    if k == 0:
        total = jnp.zeros((CX, LANES), F32)
        for a in range(NVAR):
            edge = coupling[3, :, lane_tile(k)] * values[a]
            total = jnp.where(lane == a, pltpu.roll(edge, a, 1) if a else edge, total)
        left[...] = total
    if k == TILES - 1:
        total = jnp.zeros((CX, LANES), F32)
        for a in range(NVAR):
            edge = coupling[2, :, lane_tile(k)] * values[a]
            total = jnp.where(lane == a, pltpu.roll(edge, a + 1, 1), total)
        right[...] = total


def first_kernel(rhs, inverse, coupling, out, low, high, left, right):
    for edge in (low, high):
        edge[...] = jnp.zeros_like(edge)
    for k in range(TILES):
        values = product(inverse, [rhs[b, :, lane_tile(k)] for b in range(NVAR)], k)
        for a in range(NVAR):
            out[a, :, lane_tile(k)] = values[a]
        store_edges(values, coupling, k, low, high, left, right)


def neighbour_terms(rhs, coupling, field, above, below, after, before):
    at = lax.axis_index("span")
    row = lax.broadcasted_iota(jnp.int32, (CX, LANES), 0)
    lane = lax.broadcasted_iota(jnp.int32, (CX, LANES), 1)
    after_rolled = {}
    before_rolled = {}

    def roll_back(k, b):
        if (k, b) not in after_rolled:
            if k == TILES:
                after_rolled[k, b] = pltpu.roll(after[...], LANES - 1 - b, 1)
            else:
                part = coupling[3, :, lane_tile(k)] * field[b, :, lane_tile(k)]
                after_rolled[k, b] = pltpu.roll(part, LANES - 1, 1)
        return after_rolled[k, b]

    def roll_on(k, b):
        if (k, b) not in before_rolled:
            if k < 0:
                before_rolled[k, b] = pltpu.roll(before[...], LANES - b, 1) if b else before[...]
            else:
                part = coupling[2, :, lane_tile(k)] * field[b, :, lane_tile(k)]
                before_rolled[k, b] = pltpu.roll(part, 1, 1)
        return before_rolled[k, b]

    def tile(k):
        terms = []
        for b in range(NVAR):
            value = field[b, :, lane_tile(k)]
            up = pltpu.roll(coupling[1, :, lane_tile(k)] * value, CX - 1, 0)
            edge = jnp.where(at == N_SPAN - 1, 0.0, above[b : b + 1, lane_tile(k)])
            total = jnp.where(row == CX - 1, edge, up)
            down = pltpu.roll(coupling[0, :, lane_tile(k)] * value, 1, 0)
            edge = jnp.where(at == 0, 0.0, below[b : b + 1, lane_tile(k)])
            total = total + jnp.where(row == 0, edge, down)
            total = total + jnp.where(lane == LANES - 1, roll_back(k + 1, b), roll_back(k, b))
            total = total + jnp.where(lane == 0, roll_on(k - 1, b), roll_on(k, b))
            terms.append(rhs[b, :, lane_tile(k)] - total)
        return terms

    return tile


def sweep_kernel(
    rhs, inverse, coupling, field, above, below, after, before, out, low, high, left, right
):
    for edge in (low, high):
        edge[...] = jnp.zeros_like(edge)
    terms = neighbour_terms(rhs, coupling, field, above, below, after, before)
    for k in range(TILES):
        values = product(inverse, terms(k), k)
        for a in range(NVAR):
            out[a, :, lane_tile(k)] = values[a]
        store_edges(values, coupling, k, low, high, left, right)


def last_kernel(rhs, inverse, coupling, field, above, below, after, before, grad, out, sens):
    terms = neighbour_terms(rhs, coupling, field, above, below, after, before)
    for k in range(TILES):
        values = product(inverse, terms(k), k)
        for a in range(NVAR):
            out[a, :, lane_tile(k)] = values[a]
        sens[:, lane_tile(k)] = grad[0, :, lane_tile(k)] * values[NVAR - 1]


EDGES = (f32(8, CY), f32(8, CY), f32(CX, LANES), f32(CX, LANES))


def shifted(axis, size, step):
    return [(i, (i + step) % size) for i in range(size)]


def exchange(low, high, left, right):
    above = lax.ppermute(low, "span", shifted("span", N_SPAN, -1))
    below = lax.ppermute(high, "span", shifted("span", N_SPAN, 1))
    after = lax.ppermute(left, "dom", shifted("dom", N_DOM, -1))
    before = lax.ppermute(right, "dom", shifted("dom", N_DOM, 1))
    return above, below, after, before


def relax(rhs, inverse, coupling, grad):
    whole = f32(NVAR, CX, CY)
    field, *edges = pl.pallas_call(
        first_kernel,
        out_shape=(whole, *EDGES),
        in_specs=[VMEM] * 3,
        out_specs=[VMEM] * 5,
        compiler_params=PARAMS,
        name="first_product",
    )(rhs, inverse, coupling)
    for sweep in range(SWEEPS - 1):
        field, *edges = pl.pallas_call(
            sweep_kernel,
            out_shape=(whole, *EDGES),
            in_specs=[VMEM] * 8,
            out_specs=[VMEM] * 5,
            compiler_params=PARAMS,
            name="sweep",
        )(rhs, inverse, coupling, field, *exchange(*edges))
    return pl.pallas_call(
        last_kernel,
        out_shape=(whole, f32(CX, CY)),
        in_specs=[VMEM] * 9,
        out_specs=[VMEM] * 2,
        compiler_params=PARAMS,
        name="last_sweep",
    )(rhs, inverse, coupling, field, *exchange(*edges), grad)


def two_parts(value):
    high = value.astype(BF).astype(F32)
    return high, value - high


def rows_of(ref, first, count):
    return jnp.concatenate([ref[pl.ds(first + i, 1), :] for i in range(count)], axis=1)


def sixteen(row):
    return jnp.broadcast_to(row, (16, row.shape[1])).astype(BF)


def matches(index, count):
    index = sixteen(index.astype(F32))
    first = lax.broadcasted_iota(jnp.int32, index.shape, 0)
    return [(first + 16 * k).astype(F32).astype(BF) == index for k in range(count // 16)]


def one_hot(index, count):
    return jnp.concatenate(
        [jnp.where(m, jnp.array(1, BF), jnp.array(0, BF)) for m in matches(index, count)], axis=0
    )


def weighted(index, count, values):
    masks = matches(index, count)
    parts = []
    for value in values:
        for part in two_parts(value):
            part = sixteen(part)
            parts += [jnp.where(m, part, jnp.array(0, BF)) for m in masks]
    return jnp.concatenate(parts, axis=0)


def outer_sum(left, right):
    return lax.dot_general(left, right, (((1,), (1,)), ((), ())), preferred_element_type=F32)


def live_rows_kernel(slots, out, line, done):
    live = jnp.broadcast_to(slots[...].T[0:1] < CELLS, (8, SLOT_ROWS))
    ones = jnp.where(live, 1.0, 0.0).astype(BF)
    square = (SLOT_ROWS, SLOT_ROWS)
    before = lax.broadcasted_iota(jnp.int32, square, 0) < lax.broadcasted_iota(jnp.int32, square, 1)
    place = jnp.dot(ones, jnp.where(before, 1.0, 0.0).astype(BF), preferred_element_type=F32)
    place = jnp.where(live, place, -1.0)[0:1].astype(jnp.int32)
    at_place = lax.broadcasted_iota(jnp.int32, (LIVE_PAD, SLOT_ROWS), 0) == place
    row = lax.broadcasted_iota(jnp.int32, (8, SLOT_ROWS), 1)
    half = lax.broadcasted_iota(jnp.int32, (8, SLOT_ROWS), 0)
    row = jnp.where(half == 0, row >> 4, row & 15).astype(F32).astype(BF)
    found = outer_sum(row, jnp.where(at_place, 1.0, 0.0).astype(BF))
    line[...] = jnp.broadcast_to(found[0:1] * 16.0 + found[1:2], line.shape).astype(jnp.int32)
    copy = pltpu.make_async_copy(line, out, done)
    copy.start()
    copy.wait()


def live_rows(slots):
    return pl.pallas_call(
        live_rows_kernel,
        out_shape=jax.ShapeDtypeStruct((8, LIVE_PAD), jnp.int32),
        in_specs=[VMEM],
        out_specs=SMEM,
        scratch_shapes=[pltpu.VMEM((8, LIVE_PAD), jnp.int32), pltpu.SemaphoreType.DMA],
        compiler_params=PARAMS,
        name="live_rows",
    )(slots)


def gather_kernel(live, sens, slots, out, table):
    cells = jnp.concatenate([sens[:, lane_tile(k)] for k in range(TILES)], axis=0).T
    for part, half in enumerate(two_parts(cells)):
        table[part * LANES : (part + 1) * LANES, :] = half.astype(BF)
    place = lax.broadcasted_iota(jnp.int32, (LANES, GATHER_ROWS * LANES), 0)
    out[...] = jnp.zeros_like(out)

    @pl.loop(0, LIVE_ROWS // (GATHER_ROWS * GATHER_STEPS))
    def part(j):
        for step in range(GATHER_STEPS):
            base = (j * GATHER_STEPS + step) * GATHER_ROWS
            rows = [live[0, base + i] for i in range(GATHER_ROWS)]
            slot = jnp.concatenate([slots[pl.ds(row, 1), :] for row in rows], axis=1)
            high = jnp.where(slot < CELLS, ((slot >> 7) & (TILES - 1)) * CX + (slot >> 10), 512)
            picked = jnp.dot(table[...], one_hot(high, 256), preferred_element_type=F32)
            picked = picked[:LANES] + picked[LANES:]
            value = jnp.sum(
                jnp.where(place == (slot & (LANES - 1)), picked, 0.0), axis=0, keepdims=True
            )
            for i, row in enumerate(rows):
                out[pl.ds(row, 1), :] = value[:, lane_tile(i)]


def gather(live, sens, slots):
    return pl.pallas_call(
        gather_kernel,
        out_shape=f32(SLOT_ROWS, LANES),
        in_specs=[SMEM, VMEM, VMEM],
        out_specs=VMEM,
        scratch_shapes=[pltpu.VMEM((2 * LANES, 2 * LANES), BF)],
        compiler_params=PARAMS,
        name="gather_slots",
    )(live, sens, slots)


def face_kernel(values, faces, out, total):
    total[...] = jnp.zeros_like(total)

    @pl.loop(0, SLOT_ROWS // (FACE_ROWS * FACE_STEPS))
    def chunk(j):
        part = None
        for k in range(FACE_STEPS):
            first = (j * FACE_STEPS + k) * FACE_ROWS
            face = rows_of(faces, first, FACE_ROWS)
            value = rows_of(values, first, FACE_ROWS)
            step = outer_sum(
                weighted(face >> 7, FACE_HI, [value]), one_hot(face & (LANES - 1), LANES)
            )
            part = step if part is None else part + step
        total[...] += part

    out[...] = total[:FACE_HI] + total[FACE_HI:]


def face_sums(values, faces):
    return pl.pallas_call(
        face_kernel,
        out_shape=f32(FACE_HI, LANES),
        in_specs=[VMEM] * 2,
        out_specs=VMEM,
        scratch_shapes=[pltpu.VMEM((2 * FACE_HI, LANES), F32)],
        compiler_params=PARAMS,
        name="face_sums",
    )(values, faces)


def node_kernel(part0, part1, part2, part3, grad, nodes, faces, out, total):
    at = lax.axis_index("span")
    offset = jnp.where(at == 0, 0, jnp.where(at == 1, 1, jnp.where(at == 2, N_DOM - 1, N_DOM // 2)))
    base = lax.rem(lax.axis_index("dom") + offset, N_DOM) * NODE_DEV
    faces[...] = (part0[...] + part1[...]) + (part2[...] + part3[...])
    total[...] = jnp.zeros_like(total)

    @pl.loop(0, FACE_HI // (NODE_ROWS * NODE_STEPS))
    def chunk(j):
        part = None
        for step in range(NODE_STEPS):
            g = j * NODE_STEPS + step
            sens = rows_of(faces, g * NODE_ROWS, NODE_ROWS)
            size = NODE_ROWS * LANES
            columns = pl.ds(pl.multiple_of(g * size, size), size)
            for k in range(4):
                node = nodes[k : k + 1, columns] - base
                values = [grad[c, k : k + 1, columns] * sens for c in range(3)]
                product = outer_sum(
                    weighted(node >> 7, NODE_HI, values), one_hot(node & (LANES - 1), LANES)
                )
                part = product if part is None else part + product
        total[...] += part

    for c in range(3):
        high = total[(2 * c) * NODE_HI : (2 * c + 1) * NODE_HI]
        out[c] = high + total[(2 * c + 1) * NODE_HI : (2 * c + 2) * NODE_HI]


def node_sums(parts, grad, nodes):
    return pl.pallas_call(
        node_kernel,
        out_shape=(f32(FACE_HI, LANES), f32(3, NODE_HI, LANES)),
        in_specs=[VMEM] * 6,
        out_specs=[VMEM] * 2,
        scratch_shapes=[pltpu.VMEM((6 * NODE_HI, LANES), F32)],
        compiler_params=PARAMS,
        name="node_sums",
    )(*parts, grad, nodes)


def to_node_owners(turn):
    offsets = (0, 1, N_DOM - 1, N_DOM // 2)
    return [
        (s * N_DOM + d, (s + turn) % N_SPAN * N_DOM + (d + offsets[s]) % N_DOM)
        for s in range(N_SPAN)
        for d in range(N_DOM)
    ]


def shards(
    adjoint_rhs, block_inverse, coupling, distance_grad, slot_cell, slot_face, area_grad, face_nodes
):
    adjoint, cell_sens = relax(adjoint_rhs, block_inverse, coupling, distance_grad)
    slots = slot_cell.reshape(SLOT_ROWS, LANES)
    slot_vals = gather(live_rows(slots), cell_sens, slots)
    received = lax.all_to_all(slot_vals, "dom", split_axis=0, concat_axis=0, tiled=True)
    face_part = face_sums(received, slot_face.reshape(SLOT_ROWS, LANES))
    parts = [face_part] + [
        lax.ppermute(face_part, "span", shifted("span", N_SPAN, turn)) for turn in range(1, N_SPAN)
    ]
    face_sens, part = node_sums(parts, area_grad, face_nodes)
    node_sens = sum(
        lax.ppermute(part, ("span", "dom"), to_node_owners(turn)) for turn in range(N_SPAN)
    )
    return (adjoint, face_sens.reshape(FACE_DEV), node_sens.reshape(3, NODE_DEV))


def solution(mesh):
    in_specs = (
        P(None, "span", "dom"),
        P(None, None, "span", "dom"),
        P(None, "span", "dom"),
        P(None, "span", "dom"),
        P("span", "dom", None),
        P("span", "dom", None),
        P(None, None, "dom"),
        P(None, "dom"),
    )
    out_specs = (P(None, "span", "dom"), P("dom"), P(None, "dom"))
    return jax.shard_map(shards, mesh=mesh, in_specs=in_specs, out_specs=out_specs, check_vma=False)
```

```python
import jax
import jax.numpy as jnp
import numpy as np
from jax import lax
from jax.experimental import pallas as pl
from jax.experimental.pallas import tpu as pltpu
from jax.sharding import PartitionSpec as P

NVAR = 6
SWEEPS = 4
CX = 32
CY = 1024
CELLS = 32768
CAP = 2048
FACE_DEV = 8192
NODE_DEV = 4096
N_SPAN = 4
N_DOM = 32
LANES = 128
TILES = CY // LANES
EXT = CY + LANES
WIDE = SWEEPS
PER_TILE = LANES // WIDE
GIVEN = NVAR * NVAR + NVAR + 4
PACKED = 2
AT_RHS = NVAR * NVAR
AT_COUPLING = AT_RHS + NVAR
AT_FIELD = AT_COUPLING + 8
SLOT_ROWS = N_DOM * CAP // LANES
LIVE_ROWS = CELLS // LANES + N_DOM
LIVE_PAD = 384
GATHER_ROWS, GATHER_STEPS = 8, 18
FACE_ROWS, FACE_STEPS = 16, 16
NODE_ROWS, NODE_STEPS = 8, 4
FACE_HI = FACE_DEV // LANES
NODE_HI = NODE_DEV // LANES

VMEM = pl.BlockSpec(memory_space=pltpu.VMEM)
SMEM = pl.BlockSpec(memory_space=pltpu.SMEM)
PARAMS = pltpu.CompilerParams(vmem_limit_bytes=40 << 20)
BF = jnp.bfloat16
F32 = jnp.float32


def f32(*shape):
    return jax.ShapeDtypeStruct(shape, F32)


def lane_tile(k):
    return slice(k * LANES, (k + 1) * LANES)


def product(inverse, terms):
    out = []
    for a in range(NVAR):
        total = inverse(0, a) * terms[0]
        for b in range(1, NVAR):
            total = total + inverse(b, a) * terms[b]
        out.append(total)
    return out


def pack_kernel(
    inverse0, rhs0, coupling0, inverse7, rhs7, coupling7, first, last
):
    group = lax.broadcasted_iota(jnp.int32, (CX, LANES), 1) // WIDE
    for inverse, rhs, coupling, start, out in (
        (inverse0, rhs0, coupling0, 0, first),
        (inverse7, rhs7, coupling7, LANES - WIDE, last),
    ):
        given = [inverse[b, a] for b in range(NVAR) for a in range(NVAR)]
        given += [rhs[b] for b in range(NVAR)] + [coupling[i] for i in range(4)]
        for t in range(PACKED):
            total = jnp.zeros((CX, LANES), F32)
            for q, value in enumerate(given[t * PER_TILE : (t + 1) * PER_TILE]):
                moved = pltpu.roll(value, (q * WIDE - start) % LANES, 1)
                total = jnp.where(group == q, moved, total)
            out[t] = total


def pack_columns(inverse, rhs, coupling):
    def specs(k):
        return [
            pl.BlockSpec((NVAR, NVAR, CX, LANES), lambda i: (0, 0, 0, k)),
            pl.BlockSpec((NVAR, CX, LANES), lambda i: (0, 0, k)),
            pl.BlockSpec((4, CX, LANES), lambda i: (0, 0, k)),
        ]

    return pl.pallas_call(
        pack_kernel,
        grid=(1,),
        out_shape=(f32(PACKED, CX, LANES),) * 2,
        in_specs=specs(0) + specs(TILES - 1),
        out_specs=[pl.BlockSpec((PACKED, CX, LANES), lambda i: (0, 0, 0))] * 2,
        compiler_params=PARAMS,
        name="pack_columns",
    )(inverse, rhs, coupling, inverse, rhs, coupling)


def first_kernel(
    rhs, inverse, coupling, after, before, rhs_rim, inverse_rim, coupling_rim, out, low, high
):
    lane = lax.broadcasted_iota(jnp.int32, (CX, LANES), 1)
    for v in range(GIVEN):
        t, q = divmod(v, PER_TILE)
        follow = pltpu.roll(after[t], -q * WIDE % LANES, 1)
        precede = pltpu.roll(before[t], LANES - WIDE - q * WIDE, 1)
        value = jnp.where(lane < LANES // 2, follow, precede)
        if v < NVAR * NVAR:
            inverse_rim[v // NVAR, v % NVAR] = value
        elif v < NVAR * (NVAR + 1):
            rhs_rim[v - NVAR * NVAR] = value
        else:
            coupling_rim[v - NVAR * (NVAR + 1)] = value

    for k in range(TILES + 1):
        at = lane_tile(k)
        if k < TILES:
            terms = [rhs[b, :, at] for b in range(NVAR)]
            values = product(lambda b, a: inverse[b, a, :, at], terms)
        else:
            terms = [rhs_rim[b] for b in range(NVAR)]
            values = product(lambda b, a: inverse_rim[b, a], terms)
        for a in range(NVAR):
            out[a, :, at] = values[a]

    for message, near, second in ((low, 0, 1), (high, CX - 1, CX - 2)):
        message[...] = jnp.zeros_like(message)
        for part, rim, at, rows in (
            (inverse, inverse_rim, 0, (near,)),
            (rhs, rhs_rim, AT_RHS, (near,)),
            (coupling, coupling_rim, AT_COUPLING, (near, second)),
        ):
            shape = rim.shape[:-2]
            for row in rows:
                for index in np.ndindex(*shape):
                    message[at : at + 1, :CY] = part[(*index, slice(row, row + 1), slice(None))]
                    message[at : at + 1, CY:] = rim[(*index, slice(row, row + 1), slice(None))]
                    at += 1
        field_rows(message, AT_FIELD, out, near, second)


def field_rows(message, at, field, near, second):
    for row in (near, second):
        for b in range(NVAR):
            message[at : at + 1, :] = field[b, row : row + 1, :]
            at += 1


def halo_tile(above, below, at, second_at, k):
    span = lax.axis_index("span")
    row = lax.broadcasted_iota(jnp.int32, (8, LANES), 0)
    tile = jnp.zeros((8, LANES), F32)
    for source, end, places in ((above, N_SPAN - 1, (0, 1)), (below, 0, (7, 6))):
        part = jnp.zeros((8, LANES), F32)
        for place, index in zip(places, (at, second_at)):
            if index is not None:
                part = jnp.where(row == place, source[index : index + 1, lane_tile(k)], part)
        tile = tile + jnp.where(span == end, 0.0, part)
    return tile


def with_halo(main, rim, halo, index, k):
    core = rim[index] if k == TILES else main[(*index, slice(None), lane_tile(k))]
    return jnp.concatenate([core, halo(index, k)], axis=0)


def sweep(rows, tiles, rhs, inverse, coupling, field, store):
    last = TILES + 1
    lane = lax.broadcasted_iota(jnp.int32, (rows, LANES), 1)
    rolled = {}

    def shifted_lanes(k, b, side):
        k = k % last
        if (k, b, side) not in rolled:
            part = coupling((3 - side,), k)[:rows] * field((b,), k)[:rows]
            rolled[k, b, side] = pltpu.roll(part, 1 if side else LANES - 1, 1)
        return rolled[k, b, side]

    for k in range(tiles):
        terms = []
        for b in range(NVAR):
            value = field((b,), k)
            size = value.shape[0]
            total = pltpu.roll(coupling((1,), k) * value, size - 1, 0)[:rows]
            total = total + pltpu.roll(coupling((0,), k) * value, 1, 0)[:rows]
            edge = lane == LANES - 1
            total = total + jnp.where(edge, shifted_lanes(k + 1, b, 0), shifted_lanes(k, b, 0))
            total = total + jnp.where(lane == 0, shifted_lanes(k - 1, b, 1), shifted_lanes(k, b, 1))
            terms.append(rhs((b,), k)[:rows] - total)
        store(k, product(lambda b, a: inverse((b, a), k)[:rows], terms))


def two_sweeps(given, rims, halos, field, field_halo, middle, tiles, store):
    def full(name):
        return lambda index, k: with_halo(
            given[name], rims[name], lambda i, t: halos[name][(*i, slice(None), lane_tile(t))], index, k
        )

    rhs, inverse, coupling = full("rhs"), full("inverse"), full("coupling")

    def before(index, k):
        (b,) = index
        return jnp.concatenate([field[b, :, lane_tile(k)], field_halo[b, :, lane_tile(k)]], axis=0)

    def keep(k, values):
        for a in range(NVAR):
            middle[a, :, lane_tile(k)] = values[a]

    sweep(CX + 8, TILES + 1, rhs, inverse, coupling, before, keep)
    sweep(CX, tiles, rhs, inverse, coupling, lambda i, k: middle[i[0], :, lane_tile(k)], store)


def middle_kernel(
    rhs, inverse, coupling, rhs_rim, inverse_rim, coupling_rim, field, above, below,
    rhs_halo, inverse_halo, coupling_halo, out, low, high, field_halo, middle,
):
    for k in range(TILES + 1):
        at = lane_tile(k)
        for b in range(NVAR):
            for a in range(NVAR):
                inverse_halo[b, a, :, at] = halo_tile(above, below, b * NVAR + a, None, k)
            rhs_halo[b, :, at] = halo_tile(above, below, AT_RHS + b, None, k)
            field_halo[b, :, at] = halo_tile(above, below, AT_FIELD + b, AT_FIELD + NVAR + b, k)
        for i in range(4):
            coupling_halo[i, :, at] = halo_tile(above, below, AT_COUPLING + i, AT_COUPLING + 4 + i, k)

    def store(k, values):
        for a in range(NVAR):
            out[a, :, lane_tile(k)] = values[a]

    two_sweeps(
        dict(rhs=rhs, inverse=inverse, coupling=coupling),
        dict(rhs=rhs_rim, inverse=inverse_rim, coupling=coupling_rim),
        dict(rhs=rhs_halo, inverse=inverse_halo, coupling=coupling_halo),
        field, field_halo, middle, TILES + 1, store,
    )
    for message, near, second in ((low, 0, 1), (high, CX - 1, CX - 2)):
        message[...] = jnp.zeros_like(message)
        field_rows(message, 0, out, near, second)


def last_kernel(
    rhs, inverse, coupling, rhs_rim, inverse_rim, coupling_rim, rhs_halo, inverse_halo,
    coupling_halo, field, above, below, grad, out, sens, field_halo, middle,
):
    for k in range(TILES + 1):
        for b in range(NVAR):
            field_halo[b, :, lane_tile(k)] = halo_tile(above, below, b, NVAR + b, k)

    def store(k, values):
        for a in range(NVAR):
            out[a, :, lane_tile(k)] = values[a]
        sens[:, lane_tile(k)] = grad[0, :, lane_tile(k)] * values[NVAR - 1]

    two_sweeps(
        dict(rhs=rhs, inverse=inverse, coupling=coupling),
        dict(rhs=rhs_rim, inverse=inverse_rim, coupling=coupling_rim),
        dict(rhs=rhs_halo, inverse=inverse_halo, coupling=coupling_halo),
        field, field_halo, middle, TILES, store,
    )


def shifted(axis, size, step):
    return [(i, (i + step) % size) for i in range(size)]


def to_span_neighbours(low, high):
    above = lax.ppermute(low, "span", shifted("span", N_SPAN, -1))
    below = lax.ppermute(high, "span", shifted("span", N_SPAN, 1))
    return above, below


def relax(rhs, inverse, coupling, grad):
    def call(kernel, name, shapes, scratch, *arrays):
        return pl.pallas_call(
            kernel,
            out_shape=shapes,
            in_specs=[VMEM] * len(arrays),
            out_specs=[VMEM] * len(shapes),
            scratch_shapes=scratch,
            compiler_params=PARAMS,
            name=name,
        )(*arrays)

    rims = (f32(NVAR, CX, LANES), f32(NVAR, NVAR, CX, LANES), f32(4, CX, LANES))
    halos = (f32(NVAR, 8, EXT), f32(NVAR, NVAR, 8, EXT), f32(4, 8, EXT))
    scratch = [pltpu.VMEM((NVAR, 8, EXT), F32), pltpu.VMEM((NVAR, CX + 8, EXT), F32)]
    first, last = pack_columns(inverse, rhs, coupling)
    after = lax.ppermute(first, "dom", shifted("dom", N_DOM, -1))
    before = lax.ppermute(last, "dom", shifted("dom", N_DOM, 1))
    given = (rhs, inverse, coupling)
    whole = f32(NVAR, CX, EXT)
    *rim, field, low, high = call(
        first_kernel, "first_product", (*rims, whole, f32(64, EXT), f32(64, EXT)), [],
        *given, after, before,
    )
    above, below = to_span_neighbours(low, high)
    *halo, field, low, high = call(
        middle_kernel, "sweeps_1_2", (*halos, whole, f32(16, EXT), f32(16, EXT)), scratch,
        *given, *rim, field, above, below,
    )
    above, below = to_span_neighbours(low, high)
    return call(
        last_kernel, "sweeps_3_4", (f32(NVAR, CX, CY), f32(CX, CY)), scratch,
        *given, *rim, *halo, field, above, below, grad,
    )


def two_parts(value):
    high = value.astype(BF).astype(F32)
    return high, value - high


def rows_of(ref, first, count):
    return jnp.concatenate([ref[pl.ds(first + i, 1), :] for i in range(count)], axis=1)


def sixteen(row):
    return jnp.broadcast_to(row, (16, row.shape[1])).astype(BF)


def matches(index, count):
    index = sixteen(index.astype(F32))
    first = lax.broadcasted_iota(jnp.int32, index.shape, 0)
    return [(first + 16 * k).astype(F32).astype(BF) == index for k in range(count // 16)]


def one_hot(index, count):
    return jnp.concatenate(
        [jnp.where(m, jnp.array(1, BF), jnp.array(0, BF)) for m in matches(index, count)], axis=0
    )


def weighted(index, count, values):
    masks = matches(index, count)
    parts = []
    for value in values:
        for part in two_parts(value):
            part = sixteen(part)
            parts += [jnp.where(m, part, jnp.array(0, BF)) for m in masks]
    return jnp.concatenate(parts, axis=0)


def outer_sum(left, right):
    return lax.dot_general(left, right, (((1,), (1,)), ((), ())), preferred_element_type=F32)


def live_rows_kernel(slots, out, line, done):
    live = jnp.broadcast_to(slots[...].T[0:1] < CELLS, (8, SLOT_ROWS))
    ones = jnp.where(live, 1.0, 0.0).astype(BF)
    square = (SLOT_ROWS, SLOT_ROWS)
    before = lax.broadcasted_iota(jnp.int32, square, 0) < lax.broadcasted_iota(jnp.int32, square, 1)
    place = jnp.dot(ones, jnp.where(before, 1.0, 0.0).astype(BF), preferred_element_type=F32)
    place = jnp.where(live, place, -1.0)[0:1].astype(jnp.int32)
    at_place = lax.broadcasted_iota(jnp.int32, (LIVE_PAD, SLOT_ROWS), 0) == place
    row = lax.broadcasted_iota(jnp.int32, (8, SLOT_ROWS), 1)
    half = lax.broadcasted_iota(jnp.int32, (8, SLOT_ROWS), 0)
    row = jnp.where(half == 0, row >> 4, row & 15).astype(F32).astype(BF)
    found = outer_sum(row, jnp.where(at_place, 1.0, 0.0).astype(BF))
    line[...] = jnp.broadcast_to(found[0:1] * 16.0 + found[1:2], line.shape).astype(jnp.int32)
    copy = pltpu.make_async_copy(line, out, done)
    copy.start()
    copy.wait()


def live_rows(slots):
    return pl.pallas_call(
        live_rows_kernel,
        out_shape=jax.ShapeDtypeStruct((8, LIVE_PAD), jnp.int32),
        in_specs=[VMEM],
        out_specs=SMEM,
        scratch_shapes=[pltpu.VMEM((8, LIVE_PAD), jnp.int32), pltpu.SemaphoreType.DMA],
        compiler_params=PARAMS,
        name="live_rows",
    )(slots)


def gather_kernel(live, sens, slots, out, table):
    cells = jnp.concatenate([sens[:, lane_tile(k)] for k in range(TILES)], axis=0).T
    for part, half in enumerate(two_parts(cells)):
        table[part * LANES : (part + 1) * LANES, :] = half.astype(BF)
    place = lax.broadcasted_iota(jnp.int32, (LANES, GATHER_ROWS * LANES), 0)
    out[...] = jnp.zeros_like(out)

    @pl.loop(0, LIVE_ROWS // (GATHER_ROWS * GATHER_STEPS))
    def part(j):
        for step in range(GATHER_STEPS):
            base = (j * GATHER_STEPS + step) * GATHER_ROWS
            rows = [live[0, base + i] for i in range(GATHER_ROWS)]
            slot = jnp.concatenate([slots[pl.ds(row, 1), :] for row in rows], axis=1)
            high = jnp.where(slot < CELLS, ((slot >> 7) & (TILES - 1)) * CX + (slot >> 10), 512)
            picked = jnp.dot(table[...], one_hot(high, 256), preferred_element_type=F32)
            picked = picked[:LANES] + picked[LANES:]
            value = jnp.sum(
                jnp.where(place == (slot & (LANES - 1)), picked, 0.0), axis=0, keepdims=True
            )
            for i, row in enumerate(rows):
                out[pl.ds(row, 1), :] = value[:, lane_tile(i)]


def gather(live, sens, slots):
    return pl.pallas_call(
        gather_kernel,
        out_shape=f32(SLOT_ROWS, LANES),
        in_specs=[SMEM, VMEM, VMEM],
        out_specs=VMEM,
        scratch_shapes=[pltpu.VMEM((2 * LANES, 2 * LANES), BF)],
        compiler_params=PARAMS,
        name="gather_slots",
    )(live, sens, slots)


def face_kernel(values, faces, out, total):
    total[...] = jnp.zeros_like(total)

    @pl.loop(0, SLOT_ROWS // (FACE_ROWS * FACE_STEPS))
    def chunk(j):
        part = None
        for k in range(FACE_STEPS):
            first = (j * FACE_STEPS + k) * FACE_ROWS
            face = rows_of(faces, first, FACE_ROWS)
            value = rows_of(values, first, FACE_ROWS)
            step = outer_sum(
                weighted(face >> 7, FACE_HI, [value]), one_hot(face & (LANES - 1), LANES)
            )
            part = step if part is None else part + step
        total[...] += part

    out[...] = total[:FACE_HI] + total[FACE_HI:]


def face_sums(values, faces):
    return pl.pallas_call(
        face_kernel,
        out_shape=f32(FACE_HI, LANES),
        in_specs=[VMEM] * 2,
        out_specs=VMEM,
        scratch_shapes=[pltpu.VMEM((2 * FACE_HI, LANES), F32)],
        compiler_params=PARAMS,
        name="face_sums",
    )(values, faces)


def node_kernel(part0, part1, part2, part3, grad, nodes, faces, out, total):
    at = lax.axis_index("span")
    offset = jnp.where(at == 0, 0, jnp.where(at == 1, 1, jnp.where(at == 2, N_DOM - 1, N_DOM // 2)))
    base = lax.rem(lax.axis_index("dom") + offset, N_DOM) * NODE_DEV
    faces[...] = (part0[...] + part1[...]) + (part2[...] + part3[...])
    total[...] = jnp.zeros_like(total)

    @pl.loop(0, FACE_HI // (NODE_ROWS * NODE_STEPS))
    def chunk(j):
        part = None
        for step in range(NODE_STEPS):
            g = j * NODE_STEPS + step
            sens = rows_of(faces, g * NODE_ROWS, NODE_ROWS)
            size = NODE_ROWS * LANES
            columns = pl.ds(pl.multiple_of(g * size, size), size)
            for k in range(4):
                node = nodes[k : k + 1, columns] - base
                values = [grad[c, k : k + 1, columns] * sens for c in range(3)]
                product = outer_sum(
                    weighted(node >> 7, NODE_HI, values), one_hot(node & (LANES - 1), LANES)
                )
                part = product if part is None else part + product
        total[...] += part

    for c in range(3):
        high = total[(2 * c) * NODE_HI : (2 * c + 1) * NODE_HI]
        out[c] = high + total[(2 * c + 1) * NODE_HI : (2 * c + 2) * NODE_HI]


def node_sums(parts, grad, nodes):
    return pl.pallas_call(
        node_kernel,
        out_shape=(f32(FACE_HI, LANES), f32(3, NODE_HI, LANES)),
        in_specs=[VMEM] * 6,
        out_specs=[VMEM] * 2,
        scratch_shapes=[pltpu.VMEM((6 * NODE_HI, LANES), F32)],
        compiler_params=PARAMS,
        name="node_sums",
    )(*parts, grad, nodes)


def to_node_owners(turn):
    offsets = (0, 1, N_DOM - 1, N_DOM // 2)
    return [
        (s * N_DOM + d, (s + turn) % N_SPAN * N_DOM + (d + offsets[s]) % N_DOM)
        for s in range(N_SPAN)
        for d in range(N_DOM)
    ]


def shards(
    adjoint_rhs, block_inverse, coupling, distance_grad, slot_cell, slot_face, area_grad, face_nodes
):
    adjoint, cell_sens = relax(adjoint_rhs, block_inverse, coupling, distance_grad)
    slots = slot_cell.reshape(SLOT_ROWS, LANES)
    slot_vals = gather(live_rows(slots), cell_sens, slots)
    received = lax.all_to_all(slot_vals, "dom", split_axis=0, concat_axis=0, tiled=True)
    face_part = face_sums(received, slot_face.reshape(SLOT_ROWS, LANES))
    parts = [face_part] + [
        lax.ppermute(face_part, "span", shifted("span", N_SPAN, turn)) for turn in range(1, N_SPAN)
    ]
    face_sens, part = node_sums(parts, area_grad, face_nodes)
    node_sens = sum(
        lax.ppermute(part, ("span", "dom"), to_node_owners(turn)) for turn in range(N_SPAN)
    )
    return (adjoint, face_sens.reshape(FACE_DEV), node_sens.reshape(3, NODE_DEV))


def solution(mesh):
    in_specs = (
        P(None, "span", "dom"),
        P(None, None, "span", "dom"),
        P(None, "span", "dom"),
        P(None, "span", "dom"),
        P("span", "dom", None),
        P("span", "dom", None),
        P(None, None, "dom"),
        P(None, "dom"),
    )
    out_specs = (P(None, "span", "dom"), P("dom"), P(None, "dom"))
    return jax.shard_map(shards, mesh=mesh, in_specs=in_specs, out_specs=out_specs, check_vma=False)
```

```python
import jax
import jax.numpy as jnp
import numpy as np
from jax import lax
from jax.experimental import pallas as pl
from jax.experimental.pallas import tpu as pltpu
from jax.sharding import PartitionSpec as P

NVAR = 6
SWEEPS = 4
CX = 32
CY = 1024
CELLS = 32768
CAP = 2048
FACE_DEV = 8192
NODE_DEV = 4096
N_SPAN = 4
N_DOM = 32
LANES = 128
TILES = CY // LANES
EXT = CY + LANES
WIDE = SWEEPS
PER_TILE = LANES // WIDE
GIVEN = NVAR * NVAR + NVAR + 4
PACKED = 2
AT_RHS = NVAR * NVAR
AT_COUPLING = AT_RHS + NVAR
GIVEN_ROWS = AT_COUPLING + 8
RAW_ROWS = 56
AT_RIM = 2 * NVAR * (TILES + 1)
FIELD_ROWS = 112
FIRST_ROWS = 160
SLOT_ROWS = N_DOM * CAP // LANES
LIVE_ROWS = CELLS // LANES + N_DOM
LIVE_PAD = 384
GATHER_ROWS, GATHER_STEPS = 8, 18
FACE_ROWS, FACE_STEPS = 16, 16
NODE_ROWS, NODE_STEPS = 8, 4
FACE_HI = FACE_DEV // LANES
NODE_HI = NODE_DEV // LANES

VMEM = pl.BlockSpec(memory_space=pltpu.VMEM)
SMEM = pl.BlockSpec(memory_space=pltpu.SMEM)
ANY = pl.BlockSpec(memory_space=pl.ANY)
PARAMS = pltpu.CompilerParams(vmem_limit_bytes=40 << 20)
BF = jnp.bfloat16
F32 = jnp.float32


def f32(*shape):
    return jax.ShapeDtypeStruct(shape, F32)


def lane_tile(k):
    return slice(k * LANES, (k + 1) * LANES)


def product(inverse, terms, variables=range(NVAR)):
    out = []
    for a in variables:
        total = inverse(0, a) * terms[0]
        for b in range(1, NVAR):
            total = total + inverse(b, a) * terms[b]
        out.append(total)
    return out


def pack_kernel(rhs, inverse, coupling, first, last, low, high, *scratch):
    blocks, done = scratch[:-1], scratch[-1]
    ends = [(slice(None), lane_tile(k)) for k in (0, TILES - 1)]
    ends += [(slice(row, row + 8), slice(None)) for row in (0, CX - 8)]
    copies = []
    for end, place in enumerate(ends):
        for i, source in enumerate((inverse, rhs, coupling)):
            at = (slice(None),) * (len(source.shape) - 2) + place
            n = end * 3 + i
            copies.append(pltpu.make_async_copy(source.at[at], blocks[n], done.at[n]))
    for copy in copies:
        copy.start()
    group = lax.broadcasted_iota(jnp.int32, (CX, LANES), 1) // WIDE
    for end, (out, start) in enumerate(((first, 0), (last, LANES - WIDE))):
        for copy in copies[end * 3 : end * 3 + 3]:
            copy.wait()
        inverse, rhs, coupling = blocks[end * 3 : end * 3 + 3]
        given = [inverse[b, a] for b in range(NVAR) for a in range(NVAR)]
        given += [rhs[b] for b in range(NVAR)] + [coupling[i] for i in range(4)]
        for t in range(PACKED):
            total = jnp.zeros((CX, LANES), F32)
            for q, value in enumerate(given[t * PER_TILE : (t + 1) * PER_TILE]):
                moved = pltpu.roll(value, (q * WIDE - start) % LANES, 1)
                total = jnp.where(group == q, moved, total)
            out[t] = total
    for end, (out, near, second) in enumerate(((low, 0, 1), (high, 7, 6))):
        for copy in copies[6 + end * 3 : 9 + end * 3]:
            copy.wait()
        parts = blocks[6 + end * 3 : 9 + end * 3]
        out[GIVEN_ROWS:] = jnp.zeros((RAW_ROWS - GIVEN_ROWS, CY), F32)
        for at, (i, index, row) in enumerate(given_rows(near, second)):
            out[at : at + 1, :] = parts[i][(*index, slice(row, row + 1), slice(None))]


def load_kernel(rhs, inverse, coupling, packed, rhs_own, inverse_own, coupling_own, field, done):
    arrays = ((inverse, inverse_own), (rhs, rhs_own), (coupling, coupling_own))
    groups = [slice(row, row + 8) for row in range(0, CX, 8)]
    copies = []
    for g, rows in enumerate(groups):
        for i, (source, own) in enumerate(arrays):
            at = (slice(None),) * (len(source.shape) - 2) + (rows, slice(None))
            copies.append(pltpu.make_async_copy(source.at[at], own.at[at], done.at[g * 3 + i]))
    for copy in copies:
        copy.start()
    for g, rows in enumerate(groups):
        for copy in copies[g * 3 : g * 3 + 3]:
            copy.wait()
        for k in range(TILES):
            at = lane_tile(k)
            values = product(
                lambda b, a: inverse_own[b, a, rows, at],
                [rhs_own[b, rows, at] for b in range(NVAR)],
            )
            for a in range(NVAR):
                field[a, rows, at] = values[a]


def given_rows(near, second):
    rows = [(0, (b, a), near) for b in range(NVAR) for a in range(NVAR)]
    rows += [(1, (b,), near) for b in range(NVAR)]
    return rows + [(2, (i,), row) for row in (near, second) for i in range(4)]


def rim_kernel(field, after, before, rhs_rim, inverse_rim, coupling_rim, field_rim, low, high):
    lane = lax.broadcasted_iota(jnp.int32, (CX, LANES), 1)
    for v in range(GIVEN):
        t, q = divmod(v, PER_TILE)
        follow = pltpu.roll(after[t], -q * WIDE % LANES, 1)
        precede = pltpu.roll(before[t], LANES - WIDE - q * WIDE, 1)
        value = jnp.where(lane < LANES // 2, follow, precede)
        if v < NVAR * NVAR:
            inverse_rim[v // NVAR, v % NVAR] = value
        elif v < NVAR * (NVAR + 1):
            rhs_rim[v - NVAR * NVAR] = value
        else:
            coupling_rim[v - NVAR * (NVAR + 1)] = value
    values = product(lambda b, a: inverse_rim[b, a], [rhs_rim[b] for b in range(NVAR)])
    for a in range(NVAR):
        field_rim[a] = values[a]

    def pick(b, row, k):
        return field_rim[b, row, :] if k == TILES else field[b, row, lane_tile(k)]

    for message, near, second in ((low, 0, 1), (high, CX - 1, CX - 2)):
        field_rows(message, pick, near, second)
        parts = (inverse_rim, rhs_rim, coupling_rim)
        at = AT_RIM
        for i, index, row in given_rows(near, second):
            message[at : at + 1, :] = parts[i][(*index, slice(row, row + 1), slice(None))]
            at += 1
        message[at:] = jnp.zeros((FIRST_ROWS - at, LANES), F32)


def field_rows(message, pick, near, second):
    for i, row in enumerate((near, second)):
        for b in range(NVAR):
            for k in range(TILES + 1):
                at = field_row(i, b, k)
                message[at : at + 1, :] = pick(b, slice(row, row + 1), k)


def field_row(i, b, k):
    return (i * NVAR + b) * (TILES + 1) + k


def halo_tile(sides, near, second=None):
    span = lax.axis_index("span")
    row = lax.broadcasted_iota(jnp.int32, (8, LANES), 0)
    tile = jnp.zeros((8, LANES), F32)
    for side, end, places in zip(sides, (N_SPAN - 1, 0), ((0, 1), (7, 6))):
        part = jnp.zeros((8, LANES), F32)
        for place, pick in zip(places, (near, second)):
            if pick is not None:
                part = jnp.where(row == place, pick(side), part)
        tile = tile + jnp.where(span == end, 0.0, part)
    return tile


def field_halo_tiles(field_halo, above, below):
    for k in range(TILES + 1):
        for b in range(NVAR):
            picks = [
                lambda side, at=field_row(i, b, k): side[at : at + 1, :] for i in range(2)
            ]
            field_halo[b, :, lane_tile(k)] = halo_tile((above, below), *picks)


def sweep(rows, tiles, rhs, inverse, coupling, field, store, variables=range(NVAR)):
    last = TILES + 1
    lane = lax.broadcasted_iota(jnp.int32, (rows, LANES), 1)
    rolled = {}

    def shifted_lanes(k, b, side):
        k = k % last
        if (k, b, side) not in rolled:
            part = coupling((3 - side,), k)[:rows] * field((b,), k)[:rows]
            rolled[k, b, side] = pltpu.roll(part, 1 if side else LANES - 1, 1)
        return rolled[k, b, side]

    for k in range(tiles):
        terms = []
        for b in range(NVAR):
            value = field((b,), k)
            size = value.shape[0]
            total = pltpu.roll(coupling((1,), k) * value, size - 1, 0)[:rows]
            total = total + pltpu.roll(coupling((0,), k) * value, 1, 0)[:rows]
            edge = lane == LANES - 1
            total = total + jnp.where(edge, shifted_lanes(k + 1, b, 0), shifted_lanes(k, b, 0))
            total = total + jnp.where(lane == 0, shifted_lanes(k - 1, b, 1), shifted_lanes(k, b, 1))
            terms.append(rhs((b,), k)[:rows] - total)
        store(k, product(lambda b, a: inverse((b, a), k)[:rows], terms, variables))


def with_halos(given, rims, halos):
    def full(main, rim, halo):
        def tiles(index, k):
            edge = halo[(*index, slice(None), lane_tile(k))]
            core = rim[index] if k == TILES else main[(*index, slice(None), lane_tile(k))]
            return jnp.concatenate([core, edge], axis=0)

        return tiles

    return [full(*three) for three in zip(given, rims, halos)]


def odd_sweep(arrays, field, field_halo, middle):
    def before(index, k):
        (b,) = index
        return jnp.concatenate([field(b, k), field_halo[b, :, lane_tile(k)]], axis=0)

    def keep(k, values):
        for a in range(NVAR):
            middle[a, :, lane_tile(k)] = values[a]

    sweep(CX + 8, TILES + 1, *arrays, before, keep)


def even_sweep(tiles, arrays, middle, store, variables=range(NVAR)):
    field = lambda index, k: middle[index[0], :, lane_tile(k)]
    sweep(CX, tiles, *arrays, field, store, variables)


def middle_kernel(
    rhs, inverse, coupling, rhs_rim, inverse_rim, coupling_rim, field_rim, field, raw_above,
    raw_below, above, below, rhs_halo, inverse_halo, coupling_halo, out, low, high, field_halo, middle,
):
    field_halo_tiles(field_halo, above, below)
    for k in range(TILES + 1):
        at = lane_tile(k)

        def given(row):
            if k == TILES:
                return lambda side: side[1][AT_RIM + row : AT_RIM + row + 1, :]
            return lambda side: side[0][row : row + 1, at]

        sides = ((raw_above, above), (raw_below, below))
        for b in range(NVAR):
            for a in range(NVAR):
                inverse_halo[b, a, :, at] = halo_tile(sides, given(b * NVAR + a))
            rhs_halo[b, :, at] = halo_tile(sides, given(AT_RHS + b))
        for i in range(4):
            coupling_halo[i, :, at] = halo_tile(
                sides, given(AT_COUPLING + i), given(AT_COUPLING + 4 + i)
            )

    def store(k, values):
        for a in range(NVAR):
            out[a, :, lane_tile(k)] = values[a]

    arrays = with_halos(
        (rhs, inverse, coupling),
        (rhs_rim, inverse_rim, coupling_rim),
        (rhs_halo, inverse_halo, coupling_halo),
    )
    first = lambda b, k: field_rim[b] if k == TILES else field[b, :, lane_tile(k)]
    odd_sweep(arrays, first, field_halo, middle)
    even_sweep(TILES + 1, arrays, middle, store)
    for message, near, second in ((low, 0, 1), (high, CX - 1, CX - 2)):
        field_rows(message, lambda b, row, k: out[b, row, lane_tile(k)], near, second)
        message[AT_RIM:] = jnp.zeros((FIELD_ROWS - AT_RIM, LANES), F32)


def sens_kernel(
    rhs, inverse, coupling, rhs_rim, inverse_rim, coupling_rim, rhs_halo, inverse_halo,
    coupling_halo, field, above, below, grad, live, slots, values, middle, field_halo, sens, table,
):
    field_halo_tiles(field_halo, above, below)
    arrays = with_halos(
        (rhs, inverse, coupling),
        (rhs_rim, inverse_rim, coupling_rim),
        (rhs_halo, inverse_halo, coupling_halo),
    )

    def store(k, values):
        sens[:, lane_tile(k)] = grad[0, :, lane_tile(k)] * values[0]

    odd_sweep(arrays, lambda b, k: field[b, :, lane_tile(k)], field_halo, middle)
    even_sweep(TILES, arrays, middle, store, (NVAR - 1,))
    gather_slots(live, sens, slots, values, table)


def adjoint_kernel(
    rhs, inverse, coupling, rhs_rim, inverse_rim, coupling_rim, rhs_halo, inverse_halo,
    coupling_halo, middle, out,
):
    arrays = with_halos(
        (rhs, inverse, coupling),
        (rhs_rim, inverse_rim, coupling_rim),
        (rhs_halo, inverse_halo, coupling_halo),
    )

    def store(k, values):
        for a in range(NVAR):
            out[a, :, lane_tile(k)] = values[a]

    even_sweep(TILES, arrays, middle, store)


def shifted(axis, size, step):
    return [(i, (i + step) % size) for i in range(size)]


def to_span_neighbours(low, high):
    above = lax.ppermute(low, "span", shifted("span", N_SPAN, -1))
    below = lax.ppermute(high, "span", shifted("span", N_SPAN, 1))
    return above, below


def relax_and_gather(rhs, inverse, coupling, grad, slots):
    hbm = pl.BlockSpec(memory_space=pltpu.HBM)

    def call(kernel, name, shapes, scratch, *arrays, in_specs=None, out_specs=None, cost=None):
        return pl.pallas_call(
            kernel,
            out_shape=shapes,
            in_specs=in_specs or [VMEM] * len(arrays),
            out_specs=out_specs or [VMEM] * len(shapes),
            scratch_shapes=scratch,
            compiler_params=PARAMS,
            cost_estimate=cost,
            name=name,
        )(*arrays)

    rims = (f32(NVAR, CX, LANES), f32(NVAR, NVAR, CX, LANES), f32(4, CX, LANES))
    halos = (f32(NVAR, 8, EXT), f32(NVAR, NVAR, 8, EXT), f32(4, 8, EXT))
    in_hbm = [pltpu.with_memory_space_constraint(a, pltpu.HBM) for a in (rhs, inverse, coupling)]
    blocks = [
        pltpu.VMEM((*lead, *size), F32)
        for size in ((CX, LANES),) * 2 + ((8, CY),) * 2
        for lead in ((NVAR, NVAR), (NVAR,), (4,))
    ]
    first, last, low, high = call(
        pack_kernel, "pack_given", (f32(PACKED, CX, LANES),) * 2 + (f32(RAW_ROWS, CY),) * 2,
        [*blocks, pltpu.SemaphoreType.DMA((len(blocks),))], *in_hbm, in_specs=[hbm] * 3,
    )
    after = lax.ppermute(first, "dom", shifted("dom", N_DOM, -1))
    before = lax.ppermute(last, "dom", shifted("dom", N_DOM, 1))
    *given, field = call(
        load_kernel, "load_and_product",
        (*(f32(*array.shape) for array in (rhs, inverse, coupling)), f32(NVAR, CX, CY)),
        [pltpu.SemaphoreType.DMA((3 * CX // 8,))], *in_hbm, first, in_specs=[hbm] * 3 + [ANY],
        cost=pl.CostEstimate(flops=2 * 36 * CX * CY, bytes_accessed=13 << 20, transcendentals=0),
    )
    raw = to_span_neighbours(low, high)
    live = live_rows(slots)
    *rim, low, high = call(
        rim_kernel, "rim_product",
        (*rims, f32(NVAR, CX, LANES), f32(FIRST_ROWS, LANES), f32(FIRST_ROWS, LANES)), [],
        field, after, before,
    )
    scratch = [pltpu.VMEM((NVAR, 8, EXT), F32), pltpu.VMEM((NVAR, CX + 8, EXT), F32)]
    *halo, field, low, high = call(
        middle_kernel, "sweeps_1_2",
        (*halos, f32(NVAR, CX, EXT), f32(FIELD_ROWS, LANES), f32(FIELD_ROWS, LANES)), scratch,
        *given, *rim, field, *raw, *to_span_neighbours(low, high),
    )
    arrays = (*given, *rim[:3], *halo)
    values, middle = call(
        sens_kernel, "sweep_3_and_gather",
        (f32(SLOT_ROWS, LANES), f32(NVAR, CX + 8, EXT)),
        [
            pltpu.VMEM((NVAR, 8, EXT), F32),
            pltpu.VMEM((CX, CY), F32),
            pltpu.VMEM((2 * LANES, 2 * LANES), BF),
        ],
        *arrays, field, *to_span_neighbours(low, high), grad, live, slots,
        in_specs=[VMEM] * 13 + [SMEM, VMEM],
    )
    (adjoint,) = call(adjoint_kernel, "sweep_4", (f32(NVAR, CX, CY),), [], *arrays, middle)
    return adjoint, values


def two_parts(value):
    high = value.astype(BF).astype(F32)
    return high, value - high


def rows_of(ref, first, count):
    return jnp.concatenate([ref[pl.ds(first + i, 1), :] for i in range(count)], axis=1)


def sixteen(row):
    return jnp.broadcast_to(row, (16, row.shape[1])).astype(BF)


def matches(index, count):
    index = sixteen(index.astype(F32))
    first = lax.broadcasted_iota(jnp.int32, index.shape, 0)
    return [(first + 16 * k).astype(F32).astype(BF) == index for k in range(count // 16)]


def one_hot(index, count):
    return jnp.concatenate(
        [jnp.where(m, jnp.array(1, BF), jnp.array(0, BF)) for m in matches(index, count)], axis=0
    )


def weighted(index, count, values):
    masks = matches(index, count)
    parts = []
    for value in values:
        for part in two_parts(value):
            part = sixteen(part)
            parts += [jnp.where(m, part, jnp.array(0, BF)) for m in masks]
    return jnp.concatenate(parts, axis=0)


def outer_sum(left, right):
    return lax.dot_general(left, right, (((1,), (1,)), ((), ())), preferred_element_type=F32)


def live_rows_kernel(slots, out, line, done):
    live = jnp.broadcast_to(slots[...].T[0:1] < CELLS, (8, SLOT_ROWS))
    ones = jnp.where(live, 1.0, 0.0).astype(BF)
    square = (SLOT_ROWS, SLOT_ROWS)
    before = lax.broadcasted_iota(jnp.int32, square, 0) < lax.broadcasted_iota(jnp.int32, square, 1)
    place = jnp.dot(ones, jnp.where(before, 1.0, 0.0).astype(BF), preferred_element_type=F32)
    place = jnp.where(live, place, -1.0)[0:1].astype(jnp.int32)
    at_place = lax.broadcasted_iota(jnp.int32, (LIVE_PAD, SLOT_ROWS), 0) == place
    row = lax.broadcasted_iota(jnp.int32, (8, SLOT_ROWS), 1)
    half = lax.broadcasted_iota(jnp.int32, (8, SLOT_ROWS), 0)
    row = jnp.where(half == 0, row >> 4, row & 15).astype(F32).astype(BF)
    found = outer_sum(row, jnp.where(at_place, 1.0, 0.0).astype(BF))
    line[...] = jnp.broadcast_to(found[0:1] * 16.0 + found[1:2], line.shape).astype(jnp.int32)
    copy = pltpu.make_async_copy(line, out, done)
    copy.start()
    copy.wait()


def live_rows(slots):
    return pl.pallas_call(
        live_rows_kernel,
        out_shape=jax.ShapeDtypeStruct((8, LIVE_PAD), jnp.int32),
        in_specs=[VMEM],
        out_specs=SMEM,
        scratch_shapes=[pltpu.VMEM((8, LIVE_PAD), jnp.int32), pltpu.SemaphoreType.DMA],
        compiler_params=PARAMS,
        name="live_rows",
    )(slots)


def gather_slots(live, sens, slots, out, table):
    cells = jnp.concatenate([sens[:, lane_tile(k)] for k in range(TILES)], axis=0).T
    for part, half in enumerate(two_parts(cells)):
        table[part * LANES : (part + 1) * LANES, :] = half.astype(BF)
    place = lax.broadcasted_iota(jnp.int32, (LANES, GATHER_ROWS * LANES), 0)
    out[...] = jnp.zeros_like(out)

    @pl.loop(0, LIVE_ROWS // (GATHER_ROWS * GATHER_STEPS))
    def part(j):
        for step in range(GATHER_STEPS):
            base = (j * GATHER_STEPS + step) * GATHER_ROWS
            rows = [live[0, base + i] for i in range(GATHER_ROWS)]
            slot = jnp.concatenate([slots[pl.ds(row, 1), :] for row in rows], axis=1)
            high = jnp.where(slot < CELLS, ((slot >> 7) & (TILES - 1)) * CX + (slot >> 10), 512)
            picked = jnp.dot(table[...], one_hot(high, 256), preferred_element_type=F32)
            picked = picked[:LANES] + picked[LANES:]
            value = jnp.sum(
                jnp.where(place == (slot & (LANES - 1)), picked, 0.0), axis=0, keepdims=True
            )
            for i, row in enumerate(rows):
                out[pl.ds(row, 1), :] = value[:, lane_tile(i)]


def face_kernel(values, faces, out, total):
    total[...] = jnp.zeros_like(total)

    @pl.loop(0, SLOT_ROWS // (FACE_ROWS * FACE_STEPS))
    def chunk(j):
        part = None
        for k in range(FACE_STEPS):
            first = (j * FACE_STEPS + k) * FACE_ROWS
            face = rows_of(faces, first, FACE_ROWS)
            value = rows_of(values, first, FACE_ROWS)
            step = outer_sum(
                weighted(face >> 7, FACE_HI, [value]), one_hot(face & (LANES - 1), LANES)
            )
            part = step if part is None else part + step
        total[...] += part

    out[...] = total[:FACE_HI] + total[FACE_HI:]


def face_sums(values, faces):
    return pl.pallas_call(
        face_kernel,
        out_shape=f32(FACE_HI, LANES),
        in_specs=[VMEM] * 2,
        out_specs=VMEM,
        scratch_shapes=[pltpu.VMEM((2 * FACE_HI, LANES), F32)],
        compiler_params=PARAMS,
        name="face_sums",
    )(values, faces)


def node_kernel(part0, part1, part2, part3, grad, nodes, faces, out, total):
    at = lax.axis_index("span")
    offset = jnp.where(at == 0, 0, jnp.where(at == 1, 1, jnp.where(at == 2, N_DOM - 1, N_DOM // 2)))
    base = lax.rem(lax.axis_index("dom") + offset, N_DOM) * NODE_DEV
    faces[...] = (part0[...] + part1[...]) + (part2[...] + part3[...])
    total[...] = jnp.zeros_like(total)

    @pl.loop(0, FACE_HI // (NODE_ROWS * NODE_STEPS))
    def chunk(j):
        part = None
        for step in range(NODE_STEPS):
            g = j * NODE_STEPS + step
            sens = rows_of(faces, g * NODE_ROWS, NODE_ROWS)
            size = NODE_ROWS * LANES
            columns = pl.ds(pl.multiple_of(g * size, size), size)
            for k in range(4):
                node = nodes[k : k + 1, columns] - base
                values = [grad[c, k : k + 1, columns] * sens for c in range(3)]
                product = outer_sum(
                    weighted(node >> 7, NODE_HI, values), one_hot(node & (LANES - 1), LANES)
                )
                part = product if part is None else part + product
        total[...] += part

    for c in range(3):
        high = total[(2 * c) * NODE_HI : (2 * c + 1) * NODE_HI]
        out[c] = high + total[(2 * c + 1) * NODE_HI : (2 * c + 2) * NODE_HI]


def node_sums(parts, grad, nodes):
    return pl.pallas_call(
        node_kernel,
        out_shape=(f32(FACE_HI, LANES), f32(3, NODE_HI, LANES)),
        in_specs=[VMEM] * 6,
        out_specs=[VMEM] * 2,
        scratch_shapes=[pltpu.VMEM((6 * NODE_HI, LANES), F32)],
        compiler_params=PARAMS,
        name="node_sums",
    )(*parts, grad, nodes)


def add_kernel(part0, part1, part2, part3, out):
    for c in range(3):
        total = (part0[c] + part1[c]) + (part2[c] + part3[c])
        for row in range(NODE_HI):
            out[c : c + 1, lane_tile(row)] = total[row : row + 1]


def add_parts(parts):
    return pl.pallas_call(
        add_kernel,
        out_shape=f32(3, NODE_DEV),
        in_specs=[VMEM] * 4,
        out_specs=VMEM,
        compiler_params=PARAMS,
        name="add_parts",
    )(*parts)


def to_node_owners(turn):
    offsets = (0, 1, N_DOM - 1, N_DOM // 2)
    return [
        (s * N_DOM + d, (s + turn) % N_SPAN * N_DOM + (d + offsets[s]) % N_DOM)
        for s in range(N_SPAN)
        for d in range(N_DOM)
    ]


def shards(
    adjoint_rhs, block_inverse, coupling, distance_grad, slot_cell, slot_face, area_grad, face_nodes
):
    slots = slot_cell.reshape(SLOT_ROWS, LANES)
    adjoint, slot_vals = relax_and_gather(
        adjoint_rhs, block_inverse, coupling, distance_grad, slots
    )
    received = lax.all_to_all(slot_vals, "dom", split_axis=0, concat_axis=0, tiled=True)
    face_part = face_sums(received, slot_face.reshape(SLOT_ROWS, LANES))
    parts = [face_part] + [
        lax.ppermute(face_part, "span", shifted("span", N_SPAN, turn)) for turn in range(1, N_SPAN)
    ]
    face_sens, part = node_sums(parts, area_grad, face_nodes)
    parts = [
        lax.ppermute(part, ("span", "dom"), to_node_owners(turn)) for turn in (1, 2, 3, 0)
    ]
    return (adjoint, face_sens.reshape(FACE_DEV), add_parts(parts))


def solution(mesh):
    in_specs = (
        P(None, "span", "dom"),
        P(None, None, "span", "dom"),
        P(None, "span", "dom"),
        P(None, "span", "dom"),
        P("span", "dom", None),
        P("span", "dom", None),
        P(None, None, "dom"),
        P(None, "dom"),
    )
    out_specs = (P(None, "span", "dom"), P("dom"), P(None, "dom"))
    return jax.shard_map(shards, mesh=mesh, in_specs=in_specs, out_specs=out_specs, check_vma=False)
```

```python
import jax
import jax.numpy as jnp
import numpy as np
from jax import lax
from jax.experimental import pallas as pl
from jax.experimental.pallas import tpu as pltpu
from jax.sharding import PartitionSpec as P

NVAR = 6
SWEEPS = 4
CX = 32
CY = 1024
CELLS = 32768
CAP = 2048
FACE_DEV = 8192
NODE_DEV = 4096
N_SPAN = 4
N_DOM = 32
LANES = 128
TILES = CY // LANES
EXT = CY + LANES
WIDE = SWEEPS
PER_TILE = LANES // WIDE
GIVEN = NVAR * NVAR + NVAR + 4
PACKED = 2
AT_RHS = NVAR * NVAR
AT_COUPLING = AT_RHS + NVAR
GIVEN_ROWS = AT_COUPLING + 8
RAW_ROWS = 56
AT_RIM = 2 * NVAR * (TILES + 1)
FIELD_ROWS = 112
FIRST_ROWS = 160
SLOT_ROWS = N_DOM * CAP // LANES
LIVE_ROWS = CELLS // LANES + N_DOM
LIVE_PAD = 384
GATHER_ROWS, GATHER_STEPS = 8, 18
FACE_ROWS, FACE_STEPS = 16, 16
NODE_ROWS, NODE_STEPS = 8, 4
FACE_HI = FACE_DEV // LANES
NODE_HI = NODE_DEV // LANES

VMEM = pl.BlockSpec(memory_space=pltpu.VMEM)
SMEM = pl.BlockSpec(memory_space=pltpu.SMEM)
ANY = pl.BlockSpec(memory_space=pl.ANY)
PARAMS = pltpu.CompilerParams(vmem_limit_bytes=40 << 20)
INNER = pl.CostEstimate(flops=2 * 90 * CX * CY, bytes_accessed=8 << 20, transcendentals=0)
BF = jnp.bfloat16
F32 = jnp.float32


def f32(*shape):
    return jax.ShapeDtypeStruct(shape, F32)


def lane_tile(k):
    return slice(k * LANES, (k + 1) * LANES)


def product(inverse, terms, variables=range(NVAR)):
    out = []
    for a in variables:
        total = inverse(0, a) * terms[0]
        for b in range(1, NVAR):
            total = total + inverse(b, a) * terms[b]
        out.append(total)
    return out


def pack_kernel(rhs, inverse, coupling, first, last, low, high, *scratch):
    blocks, done = scratch[:-1], scratch[-1]
    ends = [(slice(None), lane_tile(k)) for k in (0, TILES - 1)]
    ends += [(slice(row, row + 8), slice(None)) for row in (0, CX - 8)]
    copies = []
    for end, place in enumerate(ends):
        for i, source in enumerate((inverse, rhs, coupling)):
            at = (slice(None),) * (len(source.shape) - 2) + place
            n = end * 3 + i
            copies.append(pltpu.make_async_copy(source.at[at], blocks[n], done.at[n]))
    for copy in copies:
        copy.start()
    group = lax.broadcasted_iota(jnp.int32, (CX, LANES), 1) // WIDE
    for end, (out, start) in enumerate(((first, 0), (last, LANES - WIDE))):
        for copy in copies[end * 3 : end * 3 + 3]:
            copy.wait()
        inverse, rhs, coupling = blocks[end * 3 : end * 3 + 3]
        given = [inverse[b, a] for b in range(NVAR) for a in range(NVAR)]
        given += [rhs[b] for b in range(NVAR)] + [coupling[i] for i in range(4)]
        for t in range(PACKED):
            total = jnp.zeros((CX, LANES), F32)
            for q, value in enumerate(given[t * PER_TILE : (t + 1) * PER_TILE]):
                moved = pltpu.roll(value, (q * WIDE - start) % LANES, 1)
                total = jnp.where(group == q, moved, total)
            out[t] = total
    for end, (out, near, second) in enumerate(((low, 0, 1), (high, 7, 6))):
        for copy in copies[6 + end * 3 : 9 + end * 3]:
            copy.wait()
        parts = blocks[6 + end * 3 : 9 + end * 3]
        out[GIVEN_ROWS:] = jnp.zeros((RAW_ROWS - GIVEN_ROWS, CY), F32)
        for at, (i, index, row) in enumerate(given_rows(near, second)):
            out[at : at + 1, :] = parts[i][(*index, slice(row, row + 1), slice(None))]


def load_kernel(rhs, inverse, coupling, packed, rhs_own, inverse_own, coupling_own, field, done):
    arrays = ((inverse, inverse_own), (rhs, rhs_own), (coupling, coupling_own))
    groups = [slice(row, row + 8) for row in range(0, CX, 8)]
    copies = []
    for g, rows in enumerate(groups):
        for i, (source, own) in enumerate(arrays):
            at = (slice(None),) * (len(source.shape) - 2) + (rows, slice(None))
            copies.append(pltpu.make_async_copy(source.at[at], own.at[at], done.at[g * 3 + i]))
    for copy in copies:
        copy.start()
    for g, rows in enumerate(groups):
        for copy in copies[g * 3 : g * 3 + 3]:
            copy.wait()
        for k in range(TILES):
            at = lane_tile(k)
            values = product(
                lambda b, a: inverse_own[b, a, rows, at],
                [rhs_own[b, rows, at] for b in range(NVAR)],
            )
            for a in range(NVAR):
                field[a, rows, at] = values[a]


def given_rows(near, second):
    rows = [(0, (b, a), near) for b in range(NVAR) for a in range(NVAR)]
    rows += [(1, (b,), near) for b in range(NVAR)]
    return rows + [(2, (i,), row) for row in (near, second) for i in range(4)]


def rim_kernel(field, after, before, rhs_rim, inverse_rim, coupling_rim, field_rim, low, high):
    lane = lax.broadcasted_iota(jnp.int32, (CX, LANES), 1)
    for v in range(GIVEN):
        t, q = divmod(v, PER_TILE)
        follow = pltpu.roll(after[t], -q * WIDE % LANES, 1)
        precede = pltpu.roll(before[t], LANES - WIDE - q * WIDE, 1)
        value = jnp.where(lane < LANES // 2, follow, precede)
        if v < NVAR * NVAR:
            inverse_rim[v // NVAR, v % NVAR] = value
        elif v < NVAR * (NVAR + 1):
            rhs_rim[v - NVAR * NVAR] = value
        else:
            coupling_rim[v - NVAR * (NVAR + 1)] = value
    values = product(lambda b, a: inverse_rim[b, a], [rhs_rim[b] for b in range(NVAR)])
    for a in range(NVAR):
        field_rim[a] = values[a]

    def pick(b, row, k):
        return field_rim[b, row, :] if k == TILES else field[b, row, lane_tile(k)]

    for message, near, second in ((low, 0, 1), (high, CX - 1, CX - 2)):
        field_rows(message, pick, near, second)
        parts = (inverse_rim, rhs_rim, coupling_rim)
        at = AT_RIM
        for i, index, row in given_rows(near, second):
            message[at : at + 1, :] = parts[i][(*index, slice(row, row + 1), slice(None))]
            at += 1
        message[at:] = jnp.zeros((FIRST_ROWS - at, LANES), F32)


def field_rows(message, pick, near, second):
    for i, row in enumerate((near, second)):
        for b in range(NVAR):
            for k in range(TILES + 1):
                at = field_row(i, b, k)
                message[at : at + 1, :] = pick(b, slice(row, row + 1), k)


def field_row(i, b, k):
    return (i * NVAR + b) * (TILES + 1) + k


def halo_tile(sides, near, second=None):
    span = lax.axis_index("span")
    row = lax.broadcasted_iota(jnp.int32, (8, LANES), 0)
    tile = jnp.zeros((8, LANES), F32)
    for side, end, places in zip(sides, (N_SPAN - 1, 0), ((0, 1), (7, 6))):
        part = jnp.zeros((8, LANES), F32)
        for place, pick in zip(places, (near, second)):
            if pick is not None:
                part = jnp.where(row == place, pick(side), part)
        tile = tile + jnp.where(span == end, 0.0, part)
    return tile


def field_halo_tiles(field_halo, above, below):
    for k in range(TILES + 1):
        for b in range(NVAR):
            picks = [
                lambda side, at=field_row(i, b, k): side[at : at + 1, :] for i in range(2)
            ]
            field_halo[b, :, lane_tile(k)] = halo_tile((above, below), *picks)


def sweep(cut, tiles, rhs, inverse, coupling, field, store, variables=range(NVAR)):
    last = TILES + 1
    rolled = {}

    def shifted_lanes(k, b, side):
        k = k % last
        if (k, b, side) not in rolled:
            part = cut(coupling((3 - side,), k)) * cut(field((b,), k))
            rolled[k, b, side] = pltpu.roll(part, 1 if side else LANES - 1, 1)
        return rolled[k, b, side]

    for k in range(tiles):
        terms = []
        for b in range(NVAR):
            value = field((b,), k)
            total = cut(pltpu.roll(coupling((1,), k) * value, value.shape[0] - 1, 0))
            total = total + cut(pltpu.roll(coupling((0,), k) * value, 1, 0))
            lane = lax.broadcasted_iota(jnp.int32, total.shape, 1)
            edge = lane == LANES - 1
            total = total + jnp.where(edge, shifted_lanes(k + 1, b, 0), shifted_lanes(k, b, 0))
            total = total + jnp.where(lane == 0, shifted_lanes(k - 1, b, 1), shifted_lanes(k, b, 1))
            terms.append(cut(rhs((b,), k)) - total)
        store(k, product(lambda b, a: cut(inverse((b, a), k)), terms, variables))


def all_rows(part):
    return part


def own_rows(part):
    return part[:CX]


def end_rows(part):
    return jnp.concatenate([part[:8], part[16:]], axis=0)


def own_tiles(main, rim):
    return lambda index, k: rim[index] if k == TILES else main[(*index, slice(None), lane_tile(k))]


def strip_tiles(own, halo):
    def tiles(index, k):
        part = own(index, k)
        edge = halo[(*index, slice(None), lane_tile(k))]
        return jnp.concatenate([part[CX - 8 :], edge, part[:8]], axis=0)

    return tiles


def with_ends(part, ends):
    row = lax.broadcasted_iota(jnp.int32, (8, LANES), 0)
    first = jnp.where(row < 4, ends[8:], part[:8])
    last = jnp.where(row < 4, part[CX - 8 :], ends[:8])
    return jnp.concatenate([first, part[8 : CX - 8], last], axis=0)


def keep_in(ref):
    def store(k, values):
        for a in range(NVAR):
            ref[a, :, lane_tile(k)] = values[a]

    return store


def tiles_of(ref):
    return lambda index, k: ref[(*index, slice(None), lane_tile(k))]


def inner_kernel(
    rhs, inverse, coupling, rhs_rim, inverse_rim, coupling_rim, field_rim, field, odd, even
):
    arrays = [own_tiles(rhs, rhs_rim), own_tiles(inverse, inverse_rim)]
    arrays.append(own_tiles(coupling, coupling_rim))
    sweep(all_rows, TILES + 1, *arrays, own_tiles(field, field_rim), keep_in(odd))
    sweep(all_rows, TILES + 1, *arrays, tiles_of(odd), keep_in(even))


def edge_kernel(
    rhs, inverse, coupling, rhs_rim, inverse_rim, coupling_rim, field_rim, field, raw_above,
    raw_below, above, below, even, live, rhs_halo, inverse_halo, coupling_halo, out, low, high,
    field_halo, strip,
):
    field_halo_tiles(field_halo, above, below)
    for k in range(TILES + 1):
        at = lane_tile(k)

        def given(row):
            if k == TILES:
                return lambda side: side[1][AT_RIM + row : AT_RIM + row + 1, :]
            return lambda side: side[0][row : row + 1, at]

        sides = ((raw_above, above), (raw_below, below))
        for b in range(NVAR):
            for a in range(NVAR):
                inverse_halo[b, a, :, at] = halo_tile(sides, given(b * NVAR + a))
            rhs_halo[b, :, at] = halo_tile(sides, given(AT_RHS + b))
        for i in range(4):
            coupling_halo[i, :, at] = halo_tile(
                sides, given(AT_COUPLING + i), given(AT_COUPLING + 4 + i)
            )
    arrays = [
        strip_tiles(own_tiles(rhs, rhs_rim), rhs_halo),
        strip_tiles(own_tiles(inverse, inverse_rim), inverse_halo),
        strip_tiles(own_tiles(coupling, coupling_rim), coupling_halo),
    ]

    def store(k, values):
        for a in range(NVAR):
            out[a, :, lane_tile(k)] = with_ends(even[a, :, lane_tile(k)], values[a])

    first = strip_tiles(own_tiles(field, field_rim), field_halo)
    sweep(all_rows, TILES + 1, *arrays, first, keep_in(strip))
    sweep(end_rows, TILES + 1, *arrays, tiles_of(strip), store)
    for message, near, second in ((low, 0, 1), (high, CX - 1, CX - 2)):
        field_rows(message, lambda b, row, k: out[b, row, lane_tile(k)], near, second)
        message[AT_RIM:] = jnp.zeros((FIELD_ROWS - AT_RIM, LANES), F32)


def inner_sens_kernel(
    rhs, inverse, coupling, rhs_rim, inverse_rim, coupling_rim, field, grad, odd, sens
):
    arrays = [own_tiles(rhs, rhs_rim), own_tiles(inverse, inverse_rim)]
    arrays.append(own_tiles(coupling, coupling_rim))

    def store(k, values):
        sens[:, lane_tile(k)] = grad[0, :, lane_tile(k)] * values[0]

    sweep(all_rows, TILES + 1, *arrays, tiles_of(field), keep_in(odd))
    sweep(all_rows, TILES, *arrays, tiles_of(odd), store, (NVAR - 1,))


def sens_kernel(
    rhs, inverse, coupling, rhs_rim, inverse_rim, coupling_rim, rhs_halo, inverse_halo,
    coupling_halo, field, above, below, grad, inner_sens, live_list, slots, values, strip,
    field_halo, sens, table, live, done,
):
    copy = pltpu.make_async_copy(live_list, live, done)
    copy.start()
    field_halo_tiles(field_halo, above, below)
    arrays = [
        strip_tiles(own_tiles(rhs, rhs_rim), rhs_halo),
        strip_tiles(own_tiles(inverse, inverse_rim), inverse_halo),
        strip_tiles(own_tiles(coupling, coupling_rim), coupling_halo),
    ]

    def store(k, values):
        scale = jnp.concatenate([grad[0, CX - 8 :, lane_tile(k)], grad[0, :8, lane_tile(k)]], axis=0)
        ends = scale * values[0]
        sens[:, lane_tile(k)] = with_ends(inner_sens[:, lane_tile(k)], ends)

    sweep(all_rows, TILES + 1, *arrays, strip_tiles(tiles_of(field), field_halo), keep_in(strip))
    sweep(end_rows, TILES, *arrays, tiles_of(strip), store, (NVAR - 1,))
    copy.wait()
    gather_slots(live, sens, slots, values, table)


def adjoint_kernel(
    rhs, inverse, coupling, rhs_rim, inverse_rim, coupling_rim, coupling_halo, odd, strip, out
):
    inner = [own_tiles(rhs, rhs_rim), own_tiles(inverse, inverse_rim)]

    def coupled(index, k):
        own = own_tiles(coupling, coupling_rim)(index, k)
        return jnp.concatenate([own, coupling_halo[(*index, slice(None), lane_tile(k))]], axis=0)

    def field(index, k):
        ends = strip[(*index, slice(None), lane_tile(k))]
        own = with_ends(odd[(*index, slice(None), lane_tile(k))], end_rows(ends))
        return jnp.concatenate([own, ends[8:16]], axis=0)

    sweep(own_rows, TILES, *inner, coupled, field, keep_in(out))


def shifted(axis, size, step):
    return [(i, (i + step) % size) for i in range(size)]


def to_span_neighbours(low, high):
    above = lax.ppermute(low, "span", shifted("span", N_SPAN, -1))
    below = lax.ppermute(high, "span", shifted("span", N_SPAN, 1))
    return above, below


def relax_and_gather(rhs, inverse, coupling, grad, slots):
    hbm = pl.BlockSpec(memory_space=pltpu.HBM)

    def call(kernel, name, shapes, scratch, *arrays, in_specs=None, out_specs=None, cost=None):
        return pl.pallas_call(
            kernel,
            out_shape=shapes,
            in_specs=in_specs or [VMEM] * len(arrays),
            out_specs=out_specs or [VMEM] * len(shapes),
            scratch_shapes=scratch,
            compiler_params=PARAMS,
            cost_estimate=cost,
            name=name,
        )(*arrays)

    rims = (f32(NVAR, CX, LANES), f32(NVAR, NVAR, CX, LANES), f32(4, CX, LANES))
    halos = (f32(NVAR, 8, EXT), f32(NVAR, NVAR, 8, EXT), f32(4, 8, EXT))
    in_hbm = [pltpu.with_memory_space_constraint(a, pltpu.HBM) for a in (rhs, inverse, coupling)]
    blocks = [
        pltpu.VMEM((*lead, *size), F32)
        for size in ((CX, LANES),) * 2 + ((8, CY),) * 2
        for lead in ((NVAR, NVAR), (NVAR,), (4,))
    ]
    first, last, low, high = call(
        pack_kernel, "pack_given", (f32(PACKED, CX, LANES),) * 2 + (f32(RAW_ROWS, CY),) * 2,
        [*blocks, pltpu.SemaphoreType.DMA((len(blocks),))], *in_hbm, in_specs=[hbm] * 3,
    )
    after = lax.ppermute(first, "dom", shifted("dom", N_DOM, -1))
    before = lax.ppermute(last, "dom", shifted("dom", N_DOM, 1))
    *given, field = call(
        load_kernel, "load_and_product",
        (*(f32(*array.shape) for array in (rhs, inverse, coupling)), f32(NVAR, CX, CY)),
        [pltpu.SemaphoreType.DMA((3 * CX // 8,))], *in_hbm, first, in_specs=[hbm] * 3 + [ANY],
        cost=pl.CostEstimate(flops=2 * 36 * CX * CY, bytes_accessed=13 << 20, transcendentals=0),
    )
    raw = to_span_neighbours(low, high)
    live = live_rows(slots)
    *rim, low, high = call(
        rim_kernel, "rim_product",
        (*rims, f32(NVAR, CX, LANES), f32(FIRST_ROWS, LANES), f32(FIRST_ROWS, LANES)), [],
        field, after, before,
    )
    whole, strip = f32(NVAR, CX, EXT), f32(NVAR, 24, EXT)
    field_halo = pltpu.VMEM((NVAR, 8, EXT), F32)
    arrays = (*given, *rim[:3])
    odd, even = call(inner_kernel, "inner_1_2", (whole,) * 2, [], *given, *rim, field, cost=INNER)
    *halo, field, low, high = call(
        edge_kernel, "edges_1_2",
        (*halos, whole, f32(FIELD_ROWS, LANES), f32(FIELD_ROWS, LANES)),
        [field_halo, pltpu.VMEM(strip.shape, F32)],
        *given, *rim, field, *raw, *to_span_neighbours(low, high), even, live,
    )
    odd, inner_sens = call(
        inner_sens_kernel, "inner_3", (whole, f32(CX, CY)), [], *arrays, field, grad, cost=INNER
    )
    values, strip = call(
        sens_kernel, "edges_3_and_gather", (f32(SLOT_ROWS, LANES), strip),
        [
            field_halo, pltpu.VMEM((CX, CY), F32), pltpu.VMEM((2 * LANES, 2 * LANES), BF),
            pltpu.SMEM((8, LIVE_PAD), jnp.int32), pltpu.SemaphoreType.DMA,
        ],
        *arrays, *halo, field, *to_span_neighbours(low, high), grad, inner_sens, live, slots,
    )
    (adjoint,) = call(
        adjoint_kernel, "sweep_4", (f32(NVAR, CX, CY),), [], *arrays, halo[2], odd, strip
    )
    return adjoint, values


def two_parts(value):
    high = value.astype(BF).astype(F32)
    return high, value - high


def rows_of(ref, first, count):
    return jnp.concatenate([ref[pl.ds(first + i, 1), :] for i in range(count)], axis=1)


def sixteen(row):
    return jnp.broadcast_to(row, (16, row.shape[1])).astype(BF)


def matches(index, count):
    index = sixteen(index.astype(F32))
    first = lax.broadcasted_iota(jnp.int32, index.shape, 0)
    return [(first + 16 * k).astype(F32).astype(BF) == index for k in range(count // 16)]


def one_hot(index, count):
    return jnp.concatenate(
        [jnp.where(m, jnp.array(1, BF), jnp.array(0, BF)) for m in matches(index, count)], axis=0
    )


def weighted(index, count, values):
    masks = matches(index, count)
    parts = []
    for value in values:
        for part in two_parts(value):
            part = sixteen(part)
            parts += [jnp.where(m, part, jnp.array(0, BF)) for m in masks]
    return jnp.concatenate(parts, axis=0)


def outer_sum(left, right):
    return lax.dot_general(left, right, (((1,), (1,)), ((), ())), preferred_element_type=F32)


def live_rows_kernel(slots, out):
    live = jnp.where(slots[...] < CELLS, 1.0, 0.0).astype(BF)
    first = jnp.where(lax.broadcasted_iota(jnp.int32, (16, LANES), 1) == 0, 1.0, 0.0).astype(BF)
    live = outer_sum(first, live)
    square = (SLOT_ROWS, SLOT_ROWS)
    before = lax.broadcasted_iota(jnp.int32, square, 0) < lax.broadcasted_iota(jnp.int32, square, 1)
    place = jnp.dot(
        live.astype(BF), jnp.where(before, 1.0, 0.0).astype(BF), preferred_element_type=F32
    )
    place = jnp.where(live > 0.5, place, -1.0)[0:1].astype(jnp.int32)
    at_place = lax.broadcasted_iota(jnp.int32, (LIVE_PAD, SLOT_ROWS), 0) == place
    row = lax.broadcasted_iota(jnp.int32, (8, SLOT_ROWS), 1)
    half = lax.broadcasted_iota(jnp.int32, (8, SLOT_ROWS), 0)
    row = jnp.where(half == 0, row >> 4, row & 15).astype(F32).astype(BF)
    found = outer_sum(row, jnp.where(at_place, 1.0, 0.0).astype(BF))
    out[...] = jnp.broadcast_to(found[0:1] * 16.0 + found[1:2], out.shape).astype(jnp.int32)


def live_rows(slots):
    return pl.pallas_call(
        live_rows_kernel,
        out_shape=jax.ShapeDtypeStruct((8, LIVE_PAD), jnp.int32),
        in_specs=[VMEM],
        out_specs=VMEM,
        compiler_params=PARAMS,
        name="live_rows",
    )(slots)


def gather_slots(live, sens, slots, out, table):
    cells = jnp.concatenate([sens[:, lane_tile(k)] for k in range(TILES)], axis=0).T
    for part, half in enumerate(two_parts(cells)):
        table[part * LANES : (part + 1) * LANES, :] = half.astype(BF)
    place = lax.broadcasted_iota(jnp.int32, (LANES, GATHER_ROWS * LANES), 0)
    out[...] = jnp.zeros_like(out)

    @pl.loop(0, LIVE_ROWS // (GATHER_ROWS * GATHER_STEPS))
    def part(j):
        for step in range(GATHER_STEPS):
            base = (j * GATHER_STEPS + step) * GATHER_ROWS
            rows = [live[0, base + i] for i in range(GATHER_ROWS)]
            slot = jnp.concatenate([slots[pl.ds(row, 1), :] for row in rows], axis=1)
            high = jnp.where(slot < CELLS, ((slot >> 7) & (TILES - 1)) * CX + (slot >> 10), 512)
            picked = jnp.dot(table[...], one_hot(high, 256), preferred_element_type=F32)
            picked = picked[:LANES] + picked[LANES:]
            value = jnp.sum(
                jnp.where(place == (slot & (LANES - 1)), picked, 0.0), axis=0, keepdims=True
            )
            for i, row in enumerate(rows):
                out[pl.ds(row, 1), :] = value[:, lane_tile(i)]


def face_kernel(values, faces, out, total):
    total[...] = jnp.zeros_like(total)

    @pl.loop(0, SLOT_ROWS // (FACE_ROWS * FACE_STEPS))
    def chunk(j):
        part = None
        for k in range(FACE_STEPS):
            first = (j * FACE_STEPS + k) * FACE_ROWS
            face = rows_of(faces, first, FACE_ROWS)
            value = rows_of(values, first, FACE_ROWS)
            step = outer_sum(
                weighted(face >> 7, FACE_HI, [value]), one_hot(face & (LANES - 1), LANES)
            )
            part = step if part is None else part + step
        total[...] += part

    out[...] = total[:FACE_HI] + total[FACE_HI:]


def face_sums(values, faces):
    return pl.pallas_call(
        face_kernel,
        out_shape=f32(FACE_HI, LANES),
        in_specs=[VMEM] * 2,
        out_specs=VMEM,
        scratch_shapes=[pltpu.VMEM((2 * FACE_HI, LANES), F32)],
        compiler_params=PARAMS,
        name="face_sums",
    )(values, faces)


def node_kernel(part0, part1, part2, part3, grad, nodes, faces, out, total):
    at = lax.axis_index("span")
    offset = jnp.where(at == 0, 0, jnp.where(at == 1, 1, jnp.where(at == 2, N_DOM - 1, N_DOM // 2)))
    base = lax.rem(lax.axis_index("dom") + offset, N_DOM) * NODE_DEV
    faces[...] = (part0[...] + part1[...]) + (part2[...] + part3[...])
    total[...] = jnp.zeros_like(total)

    @pl.loop(0, FACE_HI // (NODE_ROWS * NODE_STEPS))
    def chunk(j):
        part = None
        for step in range(NODE_STEPS):
            g = j * NODE_STEPS + step
            sens = rows_of(faces, g * NODE_ROWS, NODE_ROWS)
            size = NODE_ROWS * LANES
            columns = pl.ds(pl.multiple_of(g * size, size), size)
            for k in range(4):
                node = nodes[k : k + 1, columns] - base
                values = [grad[c, k : k + 1, columns] * sens for c in range(3)]
                product = outer_sum(
                    weighted(node >> 7, NODE_HI, values), one_hot(node & (LANES - 1), LANES)
                )
                part = product if part is None else part + product
        total[...] += part

    for c in range(3):
        high = total[(2 * c) * NODE_HI : (2 * c + 1) * NODE_HI]
        out[c] = high + total[(2 * c + 1) * NODE_HI : (2 * c + 2) * NODE_HI]


def node_sums(parts, grad, nodes):
    return pl.pallas_call(
        node_kernel,
        out_shape=(f32(FACE_HI, LANES), f32(3, NODE_HI, LANES)),
        in_specs=[VMEM] * 6,
        out_specs=[VMEM] * 2,
        scratch_shapes=[pltpu.VMEM((6 * NODE_HI, LANES), F32)],
        compiler_params=PARAMS,
        name="node_sums",
    )(*parts, grad, nodes)


def add_kernel(part0, part1, part2, part3, out):
    for c in range(3):
        total = (part0[c] + part1[c]) + (part2[c] + part3[c])
        for row in range(NODE_HI):
            out[c : c + 1, lane_tile(row)] = total[row : row + 1]


def add_parts(parts):
    return pl.pallas_call(
        add_kernel,
        out_shape=f32(3, NODE_DEV),
        in_specs=[VMEM] * 4,
        out_specs=VMEM,
        compiler_params=PARAMS,
        name="add_parts",
    )(*parts)


def to_node_owners(turn):
    offsets = (0, 1, N_DOM - 1, N_DOM // 2)
    return [
        (s * N_DOM + d, (s + turn) % N_SPAN * N_DOM + (d + offsets[s]) % N_DOM)
        for s in range(N_SPAN)
        for d in range(N_DOM)
    ]


def shards(
    adjoint_rhs, block_inverse, coupling, distance_grad, slot_cell, slot_face, area_grad, face_nodes
):
    slots = slot_cell.reshape(SLOT_ROWS, LANES)
    adjoint, slot_vals = relax_and_gather(
        adjoint_rhs, block_inverse, coupling, distance_grad, slots
    )
    received = lax.all_to_all(slot_vals, "dom", split_axis=0, concat_axis=0, tiled=True)
    face_part = face_sums(received, slot_face.reshape(SLOT_ROWS, LANES))
    parts = [face_part] + [
        lax.ppermute(face_part, "span", shifted("span", N_SPAN, turn)) for turn in range(1, N_SPAN)
    ]
    face_sens, part = node_sums(parts, area_grad, face_nodes)
    parts = [
        lax.ppermute(part, ("span", "dom"), to_node_owners(turn)) for turn in (0, 3, 2, 1)
    ]
    return (adjoint, face_sens.reshape(FACE_DEV), add_parts(parts))


def solution(mesh):
    in_specs = (
        P(None, "span", "dom"),
        P(None, None, "span", "dom"),
        P(None, "span", "dom"),
        P(None, "span", "dom"),
        P("span", "dom", None),
        P("span", "dom", None),
        P(None, None, "dom"),
        P(None, "dom"),
    )
    out_specs = (P(None, "span", "dom"), P("dom"), P(None, "dom"))
    return jax.shard_map(shards, mesh=mesh, in_specs=in_specs, out_specs=out_specs, check_vma=False)
```

```python
import jax
import jax.numpy as jnp
import numpy as np
from jax import lax
from jax.experimental import pallas as pl
from jax.experimental.pallas import tpu as pltpu
from jax.sharding import PartitionSpec as P

NVAR = 6
SWEEPS = 4
CX = 32
CY = 1024
CELLS = 32768
CAP = 2048
FACE_DEV = 8192
NODE_DEV = 4096
N_SPAN = 4
N_DOM = 32
LANES = 128
TILES = CY // LANES
EXT = CY + LANES
WIDE = SWEEPS
PER_TILE = LANES // WIDE
GIVEN = NVAR * NVAR + NVAR + 4
PACKED = 2
AT_RHS = NVAR * NVAR
AT_COUPLING = AT_RHS + NVAR
GIVEN_ROWS = AT_COUPLING + 5
RAW_ROWS = 48
AT_RIM = 2 * NVAR * (TILES + 1)
FIELD_ROWS = 112
FIRST_ROWS = 160
SLOT_ROWS = N_DOM * CAP // LANES
LIVE_ROWS = CELLS // LANES + N_DOM
LIVE_PAD = 384
GATHER_ROWS, GATHER_STEPS = 8, 18
FACE_ROWS, FACE_STEPS = 16, 16
NODE_ROWS, NODE_STEPS = 8, 4
FACE_HI = FACE_DEV // LANES
NODE_HI = NODE_DEV // LANES

VMEM = pl.BlockSpec(memory_space=pltpu.VMEM)
SMEM = pl.BlockSpec(memory_space=pltpu.SMEM)
ANY = pl.BlockSpec(memory_space=pl.ANY)
PARAMS = pltpu.CompilerParams(vmem_limit_bytes=40 << 20)
INNER = pl.CostEstimate(flops=2 * 90 * CX * CY, bytes_accessed=8 << 20, transcendentals=0)
BF = jnp.bfloat16
F32 = jnp.float32


def f32(*shape):
    return jax.ShapeDtypeStruct(shape, F32)


def lane_tile(k):
    return slice(k * LANES, (k + 1) * LANES)


def product(inverse, terms, variables=range(NVAR)):
    out = []
    for a in variables:
        total = inverse(0, a) * terms[0]
        for b in range(1, NVAR):
            total = total + inverse(b, a) * terms[b]
        out.append(total)
    return out


def pack_kernel(rhs, inverse, coupling, first, last, low, high, *scratch):
    blocks, done = scratch[:-1], scratch[-1]
    ends = [(slice(None), lane_tile(k)) for k in (0, TILES - 1)]
    ends += [(slice(row, row + 8), slice(None)) for row in (0, CX - 8)]
    copies = []
    for end, place in enumerate(ends):
        for i, source in enumerate((inverse, rhs, coupling)):
            at = (slice(None),) * (len(source.shape) - 2) + place
            n = end * 3 + i
            copies.append(pltpu.make_async_copy(source.at[at], blocks[n], done.at[n]))
    for copy in copies:
        copy.start()
    group = lax.broadcasted_iota(jnp.int32, (CX, LANES), 1) // WIDE
    for end, (out, start) in enumerate(((first, 0), (last, LANES - WIDE))):
        for copy in copies[end * 3 : end * 3 + 3]:
            copy.wait()
        inverse, rhs, coupling = blocks[end * 3 : end * 3 + 3]
        given = [inverse[b, a] for b in range(NVAR) for a in range(NVAR)]
        given += [rhs[b] for b in range(NVAR)] + [coupling[i] for i in range(4)]
        for t in range(PACKED):
            total = jnp.zeros((CX, LANES), F32)
            for q, value in enumerate(given[t * PER_TILE : (t + 1) * PER_TILE]):
                moved = pltpu.roll(value, (q * WIDE - start) % LANES, 1)
                total = jnp.where(group == q, moved, total)
            out[t] = total
    for end, (out, near, second) in enumerate(((low, 0, 1), (high, 7, 6))):
        for copy in copies[6 + end * 3 : 9 + end * 3]:
            copy.wait()
        parts = blocks[6 + end * 3 : 9 + end * 3]
        out[GIVEN_ROWS:] = jnp.zeros((RAW_ROWS - GIVEN_ROWS, CY), F32)
        for at, (i, index, row) in enumerate(given_rows(near, second)):
            out[at : at + 1, :] = parts[i][(*index, slice(row, row + 1), slice(None))]


def load_kernel(rhs, inverse, coupling, packed, rhs_own, inverse_own, coupling_own, field, done):
    arrays = ((inverse, inverse_own), (rhs, rhs_own), (coupling, coupling_own))
    groups = [slice(row, row + 8) for row in range(0, CX, 8)]
    copies = []
    for g, rows in enumerate(groups):
        for i, (source, own) in enumerate(arrays):
            at = (slice(None),) * (len(source.shape) - 2) + (rows, slice(None))
            copies.append(pltpu.make_async_copy(source.at[at], own.at[at], done.at[g * 3 + i]))
    for copy in copies:
        copy.start()
    for g, rows in enumerate(groups):
        for copy in copies[g * 3 : g * 3 + 3]:
            copy.wait()
        for k in range(TILES):
            at = lane_tile(k)
            values = product(
                lambda b, a: inverse_own[b, a, rows, at],
                [rhs_own[b, rows, at] for b in range(NVAR)],
            )
            for a in range(NVAR):
                field[a, rows, at] = values[a]


def given_rows(near, second):
    rows = [(0, (b, a), near) for b in range(NVAR) for a in range(NVAR)]
    rows += [(1, (b,), near) for b in range(NVAR)] + [(2, (i,), near) for i in range(4)]
    return rows + [(2, (1 if near < second else 0,), second)]


def rim_kernel(field, after, before, rhs_rim, inverse_rim, coupling_rim, field_rim, low, high):
    lane = lax.broadcasted_iota(jnp.int32, (CX, LANES), 1)
    for v in range(GIVEN):
        t, q = divmod(v, PER_TILE)
        follow = pltpu.roll(after[t], -q * WIDE % LANES, 1)
        precede = pltpu.roll(before[t], LANES - WIDE - q * WIDE, 1)
        value = jnp.where(lane < LANES // 2, follow, precede)
        if v < NVAR * NVAR:
            inverse_rim[v // NVAR, v % NVAR] = value
        elif v < NVAR * (NVAR + 1):
            rhs_rim[v - NVAR * NVAR] = value
        else:
            coupling_rim[v - NVAR * (NVAR + 1)] = value
    values = product(lambda b, a: inverse_rim[b, a], [rhs_rim[b] for b in range(NVAR)])
    for a in range(NVAR):
        field_rim[a] = values[a]

    def pick(b, row, k):
        return field_rim[b, row, :] if k == TILES else field[b, row, lane_tile(k)]

    for message, near, second in ((low, 0, 1), (high, CX - 1, CX - 2)):
        field_rows(message, pick, near, second)
        parts = (inverse_rim, rhs_rim, coupling_rim)
        at = AT_RIM
        for i, index, row in given_rows(near, second):
            message[at : at + 1, :] = parts[i][(*index, slice(row, row + 1), slice(None))]
            at += 1
        message[at:] = jnp.zeros((FIRST_ROWS - at, LANES), F32)


def field_rows(message, pick, near, second):
    for i, row in enumerate((near, second)):
        for b in range(NVAR):
            for k in range(TILES + 1):
                at = field_row(i, b, k)
                message[at : at + 1, :] = pick(b, slice(row, row + 1), k)


def field_row(i, b, k):
    return (i * NVAR + b) * (TILES + 1) + k


def halo_tile(sides, near, second=None):
    span = lax.axis_index("span")
    row = lax.broadcasted_iota(jnp.int32, (8, LANES), 0)
    tile = jnp.zeros((8, LANES), F32)
    for side, end, places in zip(sides, (N_SPAN - 1, 0), ((0, 1), (7, 6))):
        part = jnp.zeros((8, LANES), F32)
        for place, pick in zip(places, (near, second)):
            if pick is not None:
                part = jnp.where(row == place, pick(side), part)
        tile = tile + jnp.where(span == end, 0.0, part)
    return tile


def field_halo_tiles(field_halo, above, below):
    for k in range(TILES + 1):
        for b in range(NVAR):
            picks = [
                lambda side, at=field_row(i, b, k): side[at : at + 1, :] for i in range(2)
            ]
            field_halo[b, :, lane_tile(k)] = halo_tile((above, below), *picks)


def sweep(cut, tiles, rhs, inverse, coupling, field, store, variables=range(NVAR)):
    last = TILES + 1
    rolled = {}

    def shifted_lanes(k, b, side):
        k = k % last
        if (k, b, side) not in rolled:
            part = cut(coupling((3 - side,), k)) * cut(field((b,), k))
            rolled[k, b, side] = pltpu.roll(part, 1 if side else LANES - 1, 1)
        return rolled[k, b, side]

    for k in range(tiles):
        terms = []
        for b in range(NVAR):
            value = field((b,), k)
            total = cut(pltpu.roll(coupling((1,), k) * value, value.shape[0] - 1, 0))
            total = total + cut(pltpu.roll(coupling((0,), k) * value, 1, 0))
            lane = lax.broadcasted_iota(jnp.int32, total.shape, 1)
            edge = lane == LANES - 1
            total = total + jnp.where(edge, shifted_lanes(k + 1, b, 0), shifted_lanes(k, b, 0))
            total = total + jnp.where(lane == 0, shifted_lanes(k - 1, b, 1), shifted_lanes(k, b, 1))
            terms.append(cut(rhs((b,), k)) - total)
        store(k, product(lambda b, a: cut(inverse((b, a), k)), terms, variables))


def all_rows(part):
    return part


def own_rows(part):
    return part[:CX]


def end_rows(part):
    return jnp.concatenate([part[:8], part[16:]], axis=0)


def own_tiles(main, rim):
    return lambda index, k: rim[index] if k == TILES else main[(*index, slice(None), lane_tile(k))]


def strip_tiles(own, halo):
    def tiles(index, k):
        part = own(index, k)
        edge = halo[(*index, slice(None), lane_tile(k))]
        return jnp.concatenate([part[CX - 8 :], edge, part[:8]], axis=0)

    return tiles


def with_ends(part, ends):
    row = lax.broadcasted_iota(jnp.int32, (8, LANES), 0)
    first = jnp.where(row < 4, ends[8:], part[:8])
    last = jnp.where(row < 4, part[CX - 8 :], ends[:8])
    return jnp.concatenate([first, part[8 : CX - 8], last], axis=0)


def keep_in(ref):
    def store(k, values):
        for a in range(NVAR):
            ref[a, :, lane_tile(k)] = values[a]

    return store


def tiles_of(ref):
    return lambda index, k: ref[(*index, slice(None), lane_tile(k))]


def inner_kernel(
    rhs, inverse, coupling, rhs_rim, inverse_rim, coupling_rim, field_rim, field, odd, even
):
    arrays = [own_tiles(rhs, rhs_rim), own_tiles(inverse, inverse_rim)]
    arrays.append(own_tiles(coupling, coupling_rim))
    sweep(all_rows, TILES + 1, *arrays, own_tiles(field, field_rim), keep_in(odd))
    sweep(all_rows, TILES + 1, *arrays, tiles_of(odd), keep_in(even))


def edge_kernel(
    rhs, inverse, coupling, rhs_rim, inverse_rim, coupling_rim, field_rim, field, raw_above,
    raw_below, above, below, even, live, rhs_halo, inverse_halo, coupling_halo, out, low, high,
    field_halo, strip,
):
    field_halo_tiles(field_halo, above, below)
    for k in range(TILES + 1):
        at = lane_tile(k)

        def given(row):
            if k == TILES:
                return lambda side: side[1][AT_RIM + row : AT_RIM + row + 1, :]
            return lambda side: side[0][row : row + 1, at]

        sides = ((raw_above, above), (raw_below, below))
        for b in range(NVAR):
            for a in range(NVAR):
                inverse_halo[b, a, :, at] = halo_tile(sides, given(b * NVAR + a))
            rhs_halo[b, :, at] = halo_tile(sides, given(AT_RHS + b))
        for i in range(4):
            second = given(AT_COUPLING + 4) if i < 2 else None
            coupling_halo[i, :, at] = halo_tile(sides, given(AT_COUPLING + i), second)
    arrays = [
        strip_tiles(own_tiles(rhs, rhs_rim), rhs_halo),
        strip_tiles(own_tiles(inverse, inverse_rim), inverse_halo),
        strip_tiles(own_tiles(coupling, coupling_rim), coupling_halo),
    ]

    def store(k, values):
        for a in range(NVAR):
            out[a, :, lane_tile(k)] = with_ends(even[a, :, lane_tile(k)], values[a])

    first = strip_tiles(own_tiles(field, field_rim), field_halo)
    sweep(all_rows, TILES + 1, *arrays, first, keep_in(strip))
    sweep(end_rows, TILES + 1, *arrays, tiles_of(strip), store)
    for message, near, second in ((low, 0, 1), (high, CX - 1, CX - 2)):
        field_rows(message, lambda b, row, k: out[b, row, lane_tile(k)], near, second)
        message[AT_RIM:] = jnp.zeros((FIELD_ROWS - AT_RIM, LANES), F32)


def inner_sens_kernel(
    rhs, inverse, coupling, rhs_rim, inverse_rim, coupling_rim, field, grad, odd, sens
):
    arrays = [own_tiles(rhs, rhs_rim), own_tiles(inverse, inverse_rim)]
    arrays.append(own_tiles(coupling, coupling_rim))

    def store(k, values):
        sens[:, lane_tile(k)] = grad[0, :, lane_tile(k)] * values[0]

    sweep(all_rows, TILES + 1, *arrays, tiles_of(field), keep_in(odd))
    sweep(all_rows, TILES, *arrays, tiles_of(odd), store, (NVAR - 1,))


def sens_kernel(
    rhs, inverse, coupling, rhs_rim, inverse_rim, coupling_rim, rhs_halo, inverse_halo,
    coupling_halo, field, above, below, grad, inner_sens, live_list, slots, values, strip,
    field_halo, sens, table, live, done,
):
    copy = pltpu.make_async_copy(live_list, live, done)
    copy.start()
    field_halo_tiles(field_halo, above, below)
    arrays = [
        strip_tiles(own_tiles(rhs, rhs_rim), rhs_halo),
        strip_tiles(own_tiles(inverse, inverse_rim), inverse_halo),
        strip_tiles(own_tiles(coupling, coupling_rim), coupling_halo),
    ]

    def store(k, values):
        scale = jnp.concatenate([grad[0, CX - 8 :, lane_tile(k)], grad[0, :8, lane_tile(k)]], axis=0)
        ends = scale * values[0]
        sens[:, lane_tile(k)] = with_ends(inner_sens[:, lane_tile(k)], ends)

    sweep(all_rows, TILES + 1, *arrays, strip_tiles(tiles_of(field), field_halo), keep_in(strip))
    sweep(end_rows, TILES, *arrays, tiles_of(strip), store, (NVAR - 1,))
    copy.wait()
    gather_slots(live, sens, slots, values, table)


def adjoint_kernel(
    rhs, inverse, coupling, rhs_rim, inverse_rim, coupling_rim, coupling_halo, odd, strip, out
):
    inner = [own_tiles(rhs, rhs_rim), own_tiles(inverse, inverse_rim)]

    def coupled(index, k):
        own = own_tiles(coupling, coupling_rim)(index, k)
        return jnp.concatenate([own, coupling_halo[(*index, slice(None), lane_tile(k))]], axis=0)

    def field(index, k):
        ends = strip[(*index, slice(None), lane_tile(k))]
        own = with_ends(odd[(*index, slice(None), lane_tile(k))], end_rows(ends))
        return jnp.concatenate([own, ends[8:16]], axis=0)

    sweep(own_rows, TILES, *inner, coupled, field, keep_in(out))


def shifted(axis, size, step):
    return [(i, (i + step) % size) for i in range(size)]


def to_span_neighbours(low, high):
    above = lax.ppermute(low, "span", shifted("span", N_SPAN, -1))
    below = lax.ppermute(high, "span", shifted("span", N_SPAN, 1))
    return above, below


def relax_and_gather(rhs, inverse, coupling, grad, slots):
    hbm = pl.BlockSpec(memory_space=pltpu.HBM)

    def call(kernel, name, shapes, scratch, *arrays, in_specs=None, out_specs=None, cost=None):
        return pl.pallas_call(
            kernel,
            out_shape=shapes,
            in_specs=in_specs or [VMEM] * len(arrays),
            out_specs=out_specs or [VMEM] * len(shapes),
            scratch_shapes=scratch,
            compiler_params=PARAMS,
            cost_estimate=cost,
            name=name,
        )(*arrays)

    rims = (f32(NVAR, CX, LANES), f32(NVAR, NVAR, CX, LANES), f32(4, CX, LANES))
    halos = (f32(NVAR, 8, EXT), f32(NVAR, NVAR, 8, EXT), f32(4, 8, EXT))
    in_hbm = [pltpu.with_memory_space_constraint(a, pltpu.HBM) for a in (rhs, inverse, coupling)]
    blocks = [
        pltpu.VMEM((*lead, *size), F32)
        for size in ((CX, LANES),) * 2 + ((8, CY),) * 2
        for lead in ((NVAR, NVAR), (NVAR,), (4,))
    ]
    first, last, low, high = call(
        pack_kernel, "pack_given", (f32(PACKED, CX, LANES),) * 2 + (f32(RAW_ROWS, CY),) * 2,
        [*blocks, pltpu.SemaphoreType.DMA((len(blocks),))], *in_hbm, in_specs=[hbm] * 3,
    )
    after = lax.ppermute(first, "dom", shifted("dom", N_DOM, -1))
    before = lax.ppermute(last, "dom", shifted("dom", N_DOM, 1))
    *given, field = call(
        load_kernel, "load_and_product",
        (*(f32(*array.shape) for array in (rhs, inverse, coupling)), f32(NVAR, CX, CY)),
        [pltpu.SemaphoreType.DMA((3 * CX // 8,))], *in_hbm, first, in_specs=[hbm] * 3 + [ANY],
        cost=pl.CostEstimate(flops=2 * 36 * CX * CY, bytes_accessed=13 << 20, transcendentals=0),
    )
    raw = to_span_neighbours(low, high)
    live = live_rows(slots)
    *rim, low, high = call(
        rim_kernel, "rim_product",
        (*rims, f32(NVAR, CX, LANES), f32(FIRST_ROWS, LANES), f32(FIRST_ROWS, LANES)), [],
        field, after, before,
    )
    whole, strip = f32(NVAR, CX, EXT), f32(NVAR, 24, EXT)
    field_halo = pltpu.VMEM((NVAR, 8, EXT), F32)
    arrays = (*given, *rim[:3])
    odd, even = call(inner_kernel, "inner_1_2", (whole,) * 2, [], *given, *rim, field, cost=INNER)
    *halo, field, low, high = call(
        edge_kernel, "edges_1_2",
        (*halos, whole, f32(FIELD_ROWS, LANES), f32(FIELD_ROWS, LANES)),
        [field_halo, pltpu.VMEM(strip.shape, F32)],
        *given, *rim, field, *raw, *to_span_neighbours(low, high), even, live,
    )
    odd, inner_sens = call(
        inner_sens_kernel, "inner_3", (whole, f32(CX, CY)), [], *arrays, field, grad, cost=INNER
    )
    values, strip = call(
        sens_kernel, "edges_3_and_gather", (f32(SLOT_ROWS, LANES), strip),
        [
            field_halo, pltpu.VMEM((CX, CY), F32), pltpu.VMEM((2 * LANES, 2 * LANES), BF),
            pltpu.SMEM((8, LIVE_PAD), jnp.int32), pltpu.SemaphoreType.DMA,
        ],
        *arrays, *halo, field, *to_span_neighbours(low, high), grad, inner_sens, live, slots,
    )
    (adjoint,) = call(
        adjoint_kernel, "sweep_4", (f32(NVAR, CX, CY),), [], *arrays, halo[2], odd, strip
    )
    return adjoint, values


def two_parts(value):
    high = value.astype(BF).astype(F32)
    return high, value - high


def rows_of(ref, first, count):
    return jnp.concatenate([ref[pl.ds(first + i, 1), :] for i in range(count)], axis=1)


def sixteen(row):
    return jnp.broadcast_to(row, (16, row.shape[1])).astype(BF)


def matches(index, count):
    index = sixteen(index.astype(F32))
    first = lax.broadcasted_iota(jnp.int32, index.shape, 0)
    return [(first + 16 * k).astype(F32).astype(BF) == index for k in range(count // 16)]


def one_hot(index, count):
    return jnp.concatenate(
        [jnp.where(m, jnp.array(1, BF), jnp.array(0, BF)) for m in matches(index, count)], axis=0
    )


def weighted(index, count, values):
    masks = matches(index, count)
    parts = []
    for value in values:
        for part in two_parts(value):
            part = sixteen(part)
            parts += [jnp.where(m, part, jnp.array(0, BF)) for m in masks]
    return jnp.concatenate(parts, axis=0)


def outer_sum(left, right):
    return lax.dot_general(left, right, (((1,), (1,)), ((), ())), preferred_element_type=F32)


def live_rows_kernel(slots, out):
    live = jnp.where(slots[...] < CELLS, 1.0, 0.0).astype(BF)
    first = jnp.where(lax.broadcasted_iota(jnp.int32, (16, LANES), 1) == 0, 1.0, 0.0).astype(BF)
    live = outer_sum(first, live)
    square = (SLOT_ROWS, SLOT_ROWS)
    before = lax.broadcasted_iota(jnp.int32, square, 0) < lax.broadcasted_iota(jnp.int32, square, 1)
    place = jnp.dot(
        live.astype(BF), jnp.where(before, 1.0, 0.0).astype(BF), preferred_element_type=F32
    )
    place = jnp.where(live > 0.5, place, -1.0)[0:1].astype(jnp.int32)
    at_place = lax.broadcasted_iota(jnp.int32, (LIVE_PAD, SLOT_ROWS), 0) == place
    row = lax.broadcasted_iota(jnp.int32, (8, SLOT_ROWS), 1)
    half = lax.broadcasted_iota(jnp.int32, (8, SLOT_ROWS), 0)
    row = jnp.where(half == 0, row >> 4, row & 15).astype(F32).astype(BF)
    found = outer_sum(row, jnp.where(at_place, 1.0, 0.0).astype(BF))
    out[...] = jnp.broadcast_to(found[0:1] * 16.0 + found[1:2], out.shape).astype(jnp.int32)


def live_rows(slots):
    return pl.pallas_call(
        live_rows_kernel,
        out_shape=jax.ShapeDtypeStruct((8, LIVE_PAD), jnp.int32),
        in_specs=[VMEM],
        out_specs=VMEM,
        compiler_params=PARAMS,
        name="live_rows",
    )(slots)


def gather_slots(live, sens, slots, out, table):
    cells = jnp.concatenate([sens[:, lane_tile(k)] for k in range(TILES)], axis=0).T
    for part, half in enumerate(two_parts(cells)):
        table[part * LANES : (part + 1) * LANES, :] = half.astype(BF)
    place = lax.broadcasted_iota(jnp.int32, (LANES, GATHER_ROWS * LANES), 0)
    out[...] = jnp.zeros_like(out)

    @pl.loop(0, LIVE_ROWS // (GATHER_ROWS * GATHER_STEPS))
    def part(j):
        for step in range(GATHER_STEPS):
            base = (j * GATHER_STEPS + step) * GATHER_ROWS
            rows = [live[0, base + i] for i in range(GATHER_ROWS)]
            slot = jnp.concatenate([slots[pl.ds(row, 1), :] for row in rows], axis=1)
            high = jnp.where(slot < CELLS, ((slot >> 7) & (TILES - 1)) * CX + (slot >> 10), 512)
            picked = jnp.dot(table[...], one_hot(high, 256), preferred_element_type=F32)
            picked = picked[:LANES] + picked[LANES:]
            value = jnp.sum(
                jnp.where(place == (slot & (LANES - 1)), picked, 0.0), axis=0, keepdims=True
            )
            for i, row in enumerate(rows):
                out[pl.ds(row, 1), :] = value[:, lane_tile(i)]


def face_kernel(values, faces, out, total):
    total[...] = jnp.zeros_like(total)

    @pl.loop(0, SLOT_ROWS // (FACE_ROWS * FACE_STEPS))
    def chunk(j):
        part = None
        for k in range(FACE_STEPS):
            first = (j * FACE_STEPS + k) * FACE_ROWS
            face = rows_of(faces, first, FACE_ROWS)
            value = rows_of(values, first, FACE_ROWS)
            step = outer_sum(
                weighted(face >> 7, FACE_HI, [value]), one_hot(face & (LANES - 1), LANES)
            )
            part = step if part is None else part + step
        total[...] += part

    out[...] = total[:FACE_HI] + total[FACE_HI:]


def face_sums(values, faces):
    return pl.pallas_call(
        face_kernel,
        out_shape=f32(FACE_HI, LANES),
        in_specs=[VMEM] * 2,
        out_specs=VMEM,
        scratch_shapes=[pltpu.VMEM((2 * FACE_HI, LANES), F32)],
        compiler_params=PARAMS,
        name="face_sums",
    )(values, faces)


def node_kernel(part0, part1, part2, part3, grad, nodes, faces, out, total):
    at = lax.axis_index("span")
    offset = jnp.where(at == 0, 0, jnp.where(at == 1, 1, jnp.where(at == 2, N_DOM - 1, N_DOM // 2)))
    base = lax.rem(lax.axis_index("dom") + offset, N_DOM) * NODE_DEV
    faces[...] = (part0[...] + part1[...]) + (part2[...] + part3[...])
    total[...] = jnp.zeros_like(total)

    @pl.loop(0, FACE_HI // (NODE_ROWS * NODE_STEPS))
    def chunk(j):
        part = None
        for step in range(NODE_STEPS):
            g = j * NODE_STEPS + step
            sens = rows_of(faces, g * NODE_ROWS, NODE_ROWS)
            size = NODE_ROWS * LANES
            columns = pl.ds(pl.multiple_of(g * size, size), size)
            for k in range(4):
                node = nodes[k : k + 1, columns] - base
                values = [grad[c, k : k + 1, columns] * sens for c in range(3)]
                product = outer_sum(
                    weighted(node >> 7, NODE_HI, values), one_hot(node & (LANES - 1), LANES)
                )
                part = product if part is None else part + product
        total[...] += part

    for c in range(3):
        high = total[(2 * c) * NODE_HI : (2 * c + 1) * NODE_HI]
        out[c] = high + total[(2 * c + 1) * NODE_HI : (2 * c + 2) * NODE_HI]


def node_sums(parts, grad, nodes):
    return pl.pallas_call(
        node_kernel,
        out_shape=(f32(FACE_HI, LANES), f32(3, NODE_HI, LANES)),
        in_specs=[VMEM] * 6,
        out_specs=[VMEM] * 2,
        scratch_shapes=[pltpu.VMEM((6 * NODE_HI, LANES), F32)],
        compiler_params=PARAMS,
        name="node_sums",
    )(*parts, grad, nodes)


def add_kernel(part0, part1, part2, part3, out):
    for c in range(3):
        total = (part0[c] + part1[c]) + (part2[c] + part3[c])
        for row in range(NODE_HI):
            out[c : c + 1, lane_tile(row)] = total[row : row + 1]


def add_parts(parts):
    return pl.pallas_call(
        add_kernel,
        out_shape=f32(3, NODE_DEV),
        in_specs=[VMEM] * 4,
        out_specs=VMEM,
        compiler_params=PARAMS,
        name="add_parts",
    )(*parts)


def to_node_owners(turn):
    offsets = (0, 1, N_DOM - 1, N_DOM // 2)
    return [
        (s * N_DOM + d, (s + turn) % N_SPAN * N_DOM + (d + offsets[s]) % N_DOM)
        for s in range(N_SPAN)
        for d in range(N_DOM)
    ]


def shards(
    adjoint_rhs, block_inverse, coupling, distance_grad, slot_cell, slot_face, area_grad, face_nodes
):
    slots = slot_cell.reshape(SLOT_ROWS, LANES)
    adjoint, slot_vals = relax_and_gather(
        adjoint_rhs, block_inverse, coupling, distance_grad, slots
    )
    received = lax.all_to_all(slot_vals, "dom", split_axis=0, concat_axis=0, tiled=True)
    face_part = face_sums(received, slot_face.reshape(SLOT_ROWS, LANES))
    parts = [face_part] + [
        lax.ppermute(face_part, "span", shifted("span", N_SPAN, turn)) for turn in range(1, N_SPAN)
    ]
    face_sens, part = node_sums(parts, area_grad, face_nodes)
    parts = [
        lax.ppermute(part, ("span", "dom"), to_node_owners(turn)) for turn in (0, 3, 2, 1)
    ]
    return (adjoint, face_sens.reshape(FACE_DEV), add_parts(parts))


def solution(mesh):
    in_specs = (
        P(None, "span", "dom"),
        P(None, None, "span", "dom"),
        P(None, "span", "dom"),
        P(None, "span", "dom"),
        P("span", "dom", None),
        P("span", "dom", None),
        P(None, None, "dom"),
        P(None, "dom"),
    )
    out_specs = (P(None, "span", "dom"), P("dom"), P(None, "dom"))
    return jax.shard_map(shards, mesh=mesh, in_specs=in_specs, out_specs=out_specs, check_vma=False)
```
